32 devices in a mesh: gen: 4 (over z), user: 4 (over y, x), cand: 2 (over core).
Axes of the slice: x: 2, y: 2, z: 4, core: 2. Of those that a mesh axis runs over, the one named last changes fastest.
Arguments:
- states: bfloat16 [4096, 4096], P(('user', 'cand')), may hold values from -6 to 6
- norm_gain: float32 [4096], replicated, may hold values from 0.1 to 1.9
- gate_weight: bfloat16 [4096, 7168], P('user', 'gen'), may hold values from -0.09375 to 0.09375
- up_weight: bfloat16 [4096, 7168], P('user', 'gen'), may hold values from -0.09375 to 0.09375
- down_weight: bfloat16 [7168, 4096], P('gen', 'user'), may hold values from -0.0625 to 0.0625
- proj_weight: bfloat16 [4096, 1024], P('gen'), may hold values from -0.09375 to 0.09375
- private_rows: bfloat16 [4096, 1024], P(('gen', 'user')), may hold values from -6 to 6
- enc_weight: bfloat16 [1024, 1024], replicated, may hold values from -0.1875 to 0.1875
- user_ids: int32 [4096], P(('gen', 'user')), may hold values from 0 to 31
Outputs:
- votes: float32 [4, 2, 128], P(None, 'cand')
The draws below stay inside these ranges and needn't reach their ends.
Inputs may be any that keep to these rules, and one draw needn't show every extreme that they name: `user_ids`: a user is a pair of a block of 256 rows and a slot; no user has rows in two blocks.
All inputs are finite; a program needn't handle non-finite values.
Results may differ from the reference program's by a relative error of at most 0.0025.
Values may be sent and summed in bfloat16 or wider, within the bound.
A program may use at most 128 MiB of HBM per device.

```python
import jax
import jax.numpy as jnp
from jax import lax

D = 4096
FF = 7168
EMB = 1024
STEPS = 4
CAP = 8
CG = 128
ROW_DEV = 256
USERS_DEV = 32
CANDS = 1024
TOKENS = 4096
ROWS = 4096
N_USER = 4
N_CAND = 2


def with_ends(array, key, least, largest):
    index_at = [jax.random.randint(jax.random.fold_in(key, axis), (), 0, length) for axis, length in enumerate(array.shape)]
    widest = array.shape.index(max(array.shape))
    neighbour = index_at[:widest] + [(index_at[widest] + 1) % array.shape[widest]] + index_at[widest + 1:]
    return array.at[tuple(index_at)].set(least).at[tuple(neighbour)].set(largest)


def block_scale(key, shape, pieces, low, largest):
    factor_of = 1.0
    for position, shards_of in pieces:
        heights = jax.random.uniform(jax.random.fold_in(jax.random.fold_in(key, 6), position), (shards_of,), jnp.float32, low / len(pieces), largest / len(pieces))
        factor_of = factor_of * jnp.repeat(jnp.exp(heights), shape[position] // shards_of).reshape((-1,) + (1,) * (len(shape) - 1 - position))
    return factor_of


def normal_values(stream_key, shape, spread, most, cuts=(), kind=jnp.bfloat16):
    gain = block_scale(stream_key, shape, cuts, -0.22, 0.18) if cuts else 1.0
    array = jax.random.normal(stream_key, shape, jnp.float32) * spread * gain
    return jnp.minimum(jnp.maximum(array, -most), most).astype(kind)


def setup_inputs(seed: int = 0) -> dict:
    streams_of = jax.random.split(jax.random.key(seed), 10)
    return {
        "states": normal_values(streams_of[0], (TOKENS, D), 1.0, 6.0, ((0, 8),)),
        "norm_gain": jnp.clip(1.0 + 0.18 * jax.random.normal(streams_of[1], (D,), jnp.float32), 0.1, 1.9),
        "gate_weight": normal_values(streams_of[2], (D, FF), D ** -0.5, 0.09375, ((0, 4), (1, 4))),
        "up_weight": normal_values(streams_of[3], (D, FF), D ** -0.5, 0.09375, ((0, 4), (1, 4))),
        "down_weight": normal_values(streams_of[4], (FF, D), FF ** -0.5, 0.0625, ((0, 4), (1, 4))),
        "proj_weight": normal_values(streams_of[5], (D, EMB), D ** -0.5, 0.09375, ((0, 4),)),
        "private_rows": normal_values(streams_of[6], (ROWS, EMB), 1.0, 6.0, ((0, 16),)),
        "enc_weight": normal_values(streams_of[7], (EMB, EMB), EMB ** -0.5, 0.1875),
        "user_ids": with_ends(jax.random.randint(streams_of[8], (ROWS,), 0, USERS_DEV), jax.random.fold_in(streams_of[8], 1), 0, USERS_DEV - 1).astype(jnp.int32),
    }


def unit_rows(matrix):
    return (matrix * lax.rsqrt(lax.optimization_barrier(jnp.sum(matrix * matrix, axis=1, keepdims=True)) + 1e-06)).astype(jnp.bfloat16)

def reference(states, norm_gain, gate_weight, up_weight, down_weight, proj_weight, private_rows, enc_weight, user_ids):
    group_tokens = CG * STEPS

    def layer_block(block):
        values = block.astype(jnp.float32)
        normed = (values * lax.rsqrt(lax.optimization_barrier(jnp.mean(values * values, axis=1, keepdims=True)) + 1e-05) * norm_gain).astype(jnp.bfloat16)
        gate = jnp.dot(normed, gate_weight, preferred_element_type=jnp.float32)
        up_proj = jnp.dot(normed, up_weight, preferred_element_type=jnp.float32)
        hidden = (jax.nn.silu(gate) * up_proj).astype(jnp.bfloat16)
        mixed = jnp.dot(hidden, down_weight, preferred_element_type=jnp.float32)
        return lax.optimization_barrier(jnp.sum((values + mixed).reshape(CG, STEPS, D), axis=1))
    summed = lax.map(layer_block, states.reshape(TOKENS // group_tokens, group_tokens, D))
    pooled = (summed.reshape(CANDS, D) / STEPS).astype(jnp.bfloat16)
    candidate = unit_rows(jnp.dot(pooled, proj_weight, preferred_element_type=jnp.float32))
    encoded = unit_rows(jnp.dot(private_rows, enc_weight, preferred_element_type=jnp.float32))
    slab = jnp.arange(ROWS, dtype=jnp.int32) // ROW_DEV
    owner = slab * USERS_DEV + user_ids
    counts = jax.ops.segment_sum(jnp.ones((ROWS,), jnp.float32), owner, num_segments=ROWS // 8)
    row_cap = jnp.minimum(1.0, CAP / counts[owner])
    scale = CANDS / ROWS

    def vote_block(index):
        start = (index * ROW_DEV).astype(jnp.int32)
        rows_here = lax.dynamic_slice_in_dim(encoded, start, ROW_DEV, 0)
        cap_here = lax.dynamic_slice_in_dim(row_cap, start, ROW_DEV, 0)
        scores = jnp.dot(rows_here, candidate.T, preferred_element_type=jnp.float32)
        kernel = jnp.exp(scores * 60.0)
        totals = lax.optimization_barrier(jnp.sum(kernel, axis=1))
        weight_rows = cap_here / totals * scale
        return jnp.dot(weight_rows, kernel, precision=lax.Precision.HIGHEST)
    blocks = lax.map(vote_block, jnp.arange(ROWS // ROW_DEV, dtype=jnp.int32))
    votes = lax.optimization_barrier(jnp.sum(blocks, axis=0))
    return votes.reshape(N_USER, N_CAND, CG)
```

```python
import functools

import jax
import jax.numpy as jnp
from jax import lax
from jax.experimental import pallas as pl
from jax.experimental.pallas import tpu as pltpu
from jax.sharding import PartitionSpec as P

STEPS = 4
CAP = 8
USERS_DEV = 32
F32 = jnp.float32
BF16 = jnp.bfloat16
MESH = pl.DeviceIdType.MESH


def unit_rows(matrix):
    return (matrix * lax.rsqrt(jnp.sum(matrix * matrix, axis=1, keepdims=True) + 1e-06)).astype(BF16)


def pool_matrix(groups):
    rows = lax.broadcasted_iota(jnp.int32, (groups, groups * STEPS), 0)
    cols = lax.broadcasted_iota(jnp.int32, (groups, groups * STEPS), 1)
    return (cols // STEPS == rows).astype(BF16)


def greet(sizes):
    barrier = pltpu.get_barrier_semaphore()
    count = 0
    for axis, size in sizes:
        me = lax.axis_index(axis)
        for k in range(1, size):
            pl.semaphore_signal(
                barrier, inc=1, device_id={axis: lax.rem(me + k, size)}, device_id_type=MESH
            )
            count += 1
    pl.semaphore_wait(barrier, count)


def push(src, dst, send, recv, axis, peer):
    return pltpu.make_async_remote_copy(
        src_ref=src, dst_ref=dst, send_sem=send, recv_sem=recv,
        device_id={axis: peer}, device_id_type=MESH,
    )


def tail_kernel(
    n_gen, n_user, n_cand, ratio,
    ph_ref, down_ref, proj_ref, ein_ref, enc_ref, cap_ref, out_ref,
    ph_in, e_mine, e_other, sib_in, rs_out, rs_in, zr_out, zr_in, cz, call_in, kern,
    tot_out, tot_in, vote_mine, vote_u_in, vote_g_mine, vote_g_in,
    ph_s, ph_r, sib_s, sib_r, rs_s, rs_r, zr_s, zr_r, cz_s, cz_r, ca_s, ca_r,
    tot_s, tot_r, vu_s, vu_r, vg_s, vg_r,
):
    u = lax.axis_index("user")
    g = lax.axis_index("gen")
    c = lax.axis_index("cand")
    sib = lax.rem(c + 1, n_cand)
    groups = ein_ref.shape[0]
    f_part = ph_ref.shape[1]
    greet((("user", n_user), ("gen", n_gen), ("cand", n_cand)))

    def peer_u(k):
        return lax.rem(u + k, n_user)

    def peer_g(k):
        return lax.rem(g + k, n_gen)

    ph_copy = [
        push(ph_ref, ph_in.at[k - 1], ph_s.at[k - 1], ph_r.at[k - 1], "user", peer_u(k))
        for k in range(1, n_user)
    ]
    for copy in ph_copy:
        copy.start()

    def embed(hidden_sum):
        mixed = jnp.dot(hidden_sum, down_ref[...], preferred_element_type=F32).astype(BF16)
        return jnp.dot(mixed, proj_ref[...], preferred_element_type=F32)

    def split(k, full):
        own = full.reshape(n_cand, groups, full.shape[1])
        e_mine[k] = jnp.where(c == 0, own[0], own[1])
        e_other[k] = jnp.where(c == 0, own[1], own[0]).astype(BF16)

    def sib_copy(k):
        return push(e_other.at[k], sib_in.at[k], sib_s.at[k], sib_r.at[k], "cand", sib)

    def rs_copy(k):
        return push(
            rs_out.at[k - 1], rs_in.at[k - 1], rs_s.at[k - 1], rs_r.at[k - 1],
            "user", lax.rem(u + n_user - k, n_user),
        )

    def step(k, _):
        push(ph_ref, ph_in.at[k - 1], ph_s.at[k - 1], ph_r.at[k - 1], "user", peer_u(k)).wait_recv()
        split(k, embed(ph_in[k - 1]))
        sib_copy(k).start()
        return 0

    split(0, embed(ph_ref[...]))
    sib_copy(0).start()

    def both(k):
        sib_copy(k).wait_recv()
        return e_mine[k] + sib_in[k].astype(F32)

    def home(k, _):
        rs_out[k - 1] = both(k).astype(BF16)
        rs_copy(k).start()
        return 0

    lax.fori_loop(1, n_user, step, 0)
    lax.fori_loop(1, n_user, home, 0)
    total = both(0) + ein_ref[...]
    for k in range(1, n_user):
        rs_copy(k).wait_recv()
        total = total + rs_in[k - 1].astype(F32)

    share = groups // n_gen
    zr_out[...] = total.reshape(n_gen, share, total.shape[1])
    own_sum = zr_out[g]
    zr_copy = []
    for k in range(1, n_gen):
        cz[k] = zr_out[peer_g(k)].astype(BF16)
        copy = push(cz.at[k], zr_in.at[k - 1], zr_s.at[k - 1], zr_r.at[k - 1], "gen", peer_g(k))
        copy.start()
        zr_copy.append(copy)
    for k in range(1, n_gen):
        zr_copy[k - 1].wait_recv()
        own_sum = own_sum + zr_in[k - 1].astype(F32)
    own_sum = own_sum * (1.0 / STEPS)
    cz[0] = unit_rows(own_sum)

    cg_copy = []
    for k in range(1, n_gen):
        copy = push(cz.at[0], call_in.at[0, pl.ds(pl.multiple_of(g * share, share), share)],
                    cz_s.at[k - 1], cz_r.at[k - 1], "gen", peer_g(k))
        copy.start()
        cg_copy.append(copy)
    call_in[0, pl.ds(pl.multiple_of(g * share, share), share)] = cz[0]
    for copy in cg_copy:
        copy.wait_recv()
    ca_copy = []
    for k in range(1, n_user):
        copy = push(call_in.at[0], call_in.at[k], ca_s.at[k - 1], ca_r.at[k - 1], "user", peer_u(k))
        copy.start()
        ca_copy.append(copy)

    def score(k):
        scores = lax.dot_general(
            enc_ref[...], call_in[k], (((1,), (1,)), ((), ())), preferred_element_type=F32
        )
        value = jnp.exp(scores * 60.0)
        kern[k] = value
        return jnp.sum(value, axis=1, keepdims=True)

    totals = score(0)
    for k in range(1, n_user):
        ca_copy[k - 1].wait_recv()
        totals = totals + score(k)
    tot_out[...] = jnp.broadcast_to(totals, tot_out.shape)
    tot_copy = push(tot_out, tot_in, tot_s.at[0], tot_r.at[0], "cand", sib)
    tot_copy.start()
    tot_copy.wait_recv()
    totals = totals + tot_in[:, :1]
    weight = cap_ref[...] / totals * ratio
    for k in range(n_user):
        part = jnp.sum(kern[k] * weight, axis=0, keepdims=True)
        vote_mine[lax.rem(u + n_user - k, n_user)] = jnp.broadcast_to(part, vote_mine.shape[1:])

    vu_copy = []
    for k in range(1, n_user):
        copy = push(vote_mine, vote_u_in.at[k - 1], vu_s.at[k - 1], vu_r.at[k - 1], "user", peer_u(k))
        copy.start()
        vu_copy.append(copy)
    votes = vote_mine[...]
    for k in range(1, n_user):
        vu_copy[k - 1].wait_recv()
        votes = votes + vote_u_in[k - 1]
    vote_g_mine[...] = votes
    vg_copy = []
    for k in range(1, n_gen):
        copy = push(vote_g_mine, vote_g_in.at[k - 1], vg_s.at[k - 1], vg_r.at[k - 1], "gen", peer_g(k))
        copy.start()
        vg_copy.append(copy)
    for k in range(1, n_gen):
        vg_copy[k - 1].wait_recv()
        votes = votes + vote_g_in[k - 1]
    out_ref[...] = votes[:, :1, :]

    for copy in ph_copy + zr_copy + cg_copy + ca_copy + [tot_copy] + vu_copy + vg_copy:
        copy.wait_send()

    def finish(k, _):
        sib_copy(k).wait_send()
        return 0

    def finish_rs(k, _):
        rs_copy(k).wait_send()
        return 0

    lax.fori_loop(0, n_user, finish, 0)
    lax.fori_loop(1, n_user, finish_rs, 0)


def tail(hidden_sum, down_part, proj_user, e_in, encoded, row_cap, ratio):
    n_gen, n_user, n_cand = (lax.axis_size(a) for a in ("gen", "user", "cand"))
    groups, emb = e_in.shape
    rows = encoded.shape[0]
    share = groups // n_gen
    vmem = pltpu.VMEM
    dma = pltpu.SemaphoreType.DMA
    nu, ng = n_user - 1, n_gen - 1
    return pl.pallas_call(
        functools.partial(tail_kernel, n_gen, n_user, n_cand, ratio),
        out_shape=jax.ShapeDtypeStruct((n_user, 1, groups), F32),
        in_specs=[pl.BlockSpec(memory_space=vmem)] * 6,
        out_specs=pl.BlockSpec(memory_space=vmem),
        scratch_shapes=[
            vmem((nu, *hidden_sum.shape), BF16),
            vmem((n_user, groups, emb), F32),
            vmem((n_user, groups, emb), BF16),
            vmem((n_user, groups, emb), BF16),
            vmem((nu, groups, emb), BF16),
            vmem((nu, groups, emb), BF16),
            vmem((n_gen, share, emb), F32),
            vmem((ng, share, emb), BF16),
            vmem((n_gen, share, emb), BF16),
            vmem((n_user, groups, emb), BF16),
            vmem((n_user, rows, groups), F32),
            vmem((rows, 128), F32),
            vmem((rows, 128), F32),
            vmem((n_user, 8, groups), F32),
            vmem((nu, n_user, 8, groups), F32),
            vmem((n_user, 8, groups), F32),
            vmem((ng, n_user, 8, groups), F32),
            dma((nu,)), dma((nu,)),
            dma((n_user,)), dma((n_user,)),
            dma((nu,)), dma((nu,)),
            dma((ng,)), dma((ng,)),
            dma((ng,)), dma((ng,)),
            dma((nu,)), dma((nu,)),
            dma((1,)), dma((1,)),
            dma((nu,)), dma((nu,)),
            dma((ng,)), dma((ng,)),
        ],
        compiler_params=pltpu.CompilerParams(
            collective_id=0, has_side_effects=True, vmem_limit_bytes=56 * 1024 * 1024
        ),
    )(hidden_sum, down_part, proj_user, e_in, encoded, row_cap)


def project_in(inputs, gate_part, up_part):

    def add_rows(piece):
        return jnp.dot(inputs, piece, preferred_element_type=F32)

    gate = add_rows(lax.all_gather(gate_part, "user", axis=0, tiled=True))
    up_proj = add_rows(lax.all_gather(up_part, "user", axis=0, tiled=True))
    return (gate, up_proj)


def proj_of_user(proj_weight):
    n_gen, n_user = lax.axis_size("gen"), lax.axis_size("user")
    per = n_user // n_gen
    rows = proj_weight.shape[0] // per
    slot = lax.rem(lax.axis_index("user"), per)
    piece = lax.dynamic_slice_in_dim(proj_weight, slot * rows, rows, 0)
    pairs = [
        (a * n_user + b, (b // per) * n_user + a * per + b % per)
        for a in range(n_gen) for b in range(n_user)
    ]
    return lax.ppermute(piece, ("gen", "user"), pairs)


def shards(
    states,
    norm_gain,
    gate_weight,
    up_weight,
    down_weight,
    proj_weight,
    private_rows,
    enc_weight,
    user_ids,
):
    tok_rows, width_model = states.shape
    groups = tok_rows // STEPS
    values = states.astype(F32)
    normed = (
        values * lax.rsqrt(jnp.mean(values * values, axis=1, keepdims=True) + 1e-05) * norm_gain
    ).astype(BF16)
    partners = lax.axis_size("cand")
    own_part = lax.axis_index("cand")
    part_width = gate_weight.shape[1] // partners
    gate_part = lax.dynamic_slice_in_dim(gate_weight, own_part * part_width, part_width, 1)
    up_part = lax.dynamic_slice_in_dim(up_weight, own_part * part_width, part_width, 1)
    down_part = lax.dynamic_slice_in_dim(down_weight, own_part * part_width, part_width, 0)
    inputs = lax.all_gather(normed, "cand", axis=0, tiled=True)
    gate, up_proj = project_in(inputs, gate_part, up_part)
    hidden = (jax.nn.silu(gate) * up_proj).astype(BF16)
    hidden_sum = jnp.dot(
        pool_matrix(hidden.shape[0] // STEPS), hidden, preferred_element_type=F32
    ).astype(BF16)

    proj_user = proj_of_user(proj_weight)
    slab_width = proj_weight.shape[0]
    own_cols = lax.dynamic_slice_in_dim(states, lax.axis_index("gen") * slab_width, slab_width, 1)
    pooled_in = jnp.dot(pool_matrix(groups), own_cols, preferred_element_type=F32).astype(BF16)
    e_in = jnp.dot(pooled_in, proj_weight, preferred_element_type=F32)
    encoded = unit_rows(jnp.dot(private_rows, enc_weight, preferred_element_type=F32))
    member = (user_ids[:, None] == jnp.arange(USERS_DEV, dtype=jnp.int32)[None, :]).astype(F32)
    counts = jnp.sum(member, axis=0)
    limit = jnp.minimum(1.0, CAP / jnp.maximum(counts, 1.0))
    row_cap = jnp.sum(member * limit[None, :], axis=1, keepdims=True)
    row_total = private_rows.shape[0] * lax.axis_size("gen") * lax.axis_size("user")
    cand_total = groups * lax.axis_size("user") * partners
    return tail(
        hidden_sum, down_part, proj_user, e_in, encoded, row_cap, cand_total / row_total
    )


def solution(mesh):
    return jax.shard_map(
        shards,
        mesh=mesh,
        in_specs=(
            P(("user", "cand"), None),
            P(),
            P("user", "gen"),
            P("user", "gen"),
            P("gen", "user"),
            P("gen", None),
            P(("gen", "user"), None),
            P(),
            P(("gen", "user")),
        ),
        out_specs=P(None, "cand", None),
        check_vma=False,
    )
```

```python
import functools

import jax
import jax.numpy as jnp
from jax import lax
from jax.experimental import pallas as pl
from jax.experimental.pallas import tpu as pltpu
from jax.sharding import PartitionSpec as P

STEPS = 4
CAP = 8
USERS_DEV = 32
F32 = jnp.float32
BF16 = jnp.bfloat16
MESH = pl.DeviceIdType.MESH


def unit_rows(matrix):
    return (matrix * lax.rsqrt(jnp.sum(matrix * matrix, axis=1, keepdims=True) + 1e-06)).astype(BF16)


def pool_matrix(groups):
    rows = lax.broadcasted_iota(jnp.int32, (groups, groups * STEPS), 0)
    cols = lax.broadcasted_iota(jnp.int32, (groups, groups * STEPS), 1)
    return (cols // STEPS == rows).astype(BF16)


def greet(sizes):
    barrier = pltpu.get_barrier_semaphore()
    count = 0
    for axis, size in sizes:
        me = lax.axis_index(axis)
        for k in range(1, size):
            pl.semaphore_signal(
                barrier, inc=1, device_id={axis: lax.rem(me + k, size)}, device_id_type=MESH
            )
            count += 1
    pl.semaphore_wait(barrier, count)


def push(src, dst, send, recv, axis, peer):
    return pltpu.make_async_remote_copy(
        src_ref=src, dst_ref=dst, send_sem=send, recv_sem=recv,
        device_id={axis: peer}, device_id_type=MESH,
    )


def normalise(block, gain):
    values = block.astype(F32)
    scale = lax.rsqrt(jnp.mean(values * values, axis=1, keepdims=True) + 1e-05)
    return (values * scale * gain).astype(BF16)


def head_kernel(
    n_gen, n_user, n_cand, chunks,
    states_ref, gain_ref, gate_ref, up_ref, ph_ref,
    wbuf, own_norm, part_raw, part_norm, acc,
    loc, a_s, a_r, b_s, b_r, c_s, c_r, sa_s, sa_r, sb_s, sb_r, sc_s, sc_r, n_s, n_r, z_s, z_r,
):
    u = lax.axis_index("user")
    g = lax.axis_index("gen")
    c = lax.axis_index("cand")
    cols = n_user // 2
    q, x = u // 2, lax.rem(u, 2)
    mate = q * 2 + 1 - x
    gen_mate = (g // 2) * 2 + 1 - lax.rem(g, 2)
    sib = lax.rem(c + 1, n_cand)
    tokens, width = states_ref.shape
    depth, half = wbuf.shape[2], wbuf.shape[3]
    share = depth // n_cand
    mine = pl.ds(pl.multiple_of(c * share, share), share)
    weights = (gate_ref, up_ref)

    def above(dq):
        return lax.rem(q + dq, cols) * 2 + x

    barrier = pltpu.get_barrier_semaphore()
    for axis, peer in [("user", mate), ("gen", gen_mate), ("cand", sib)] + [
        ("user", above(dq)) for dq in range(1, cols)
    ]:
        pl.semaphore_signal(barrier, inc=1, device_id={axis: peer}, device_id_type=MESH)
    pl.semaphore_wait(barrier, cols + 2)

    def part(ref, which, rows):
        if len(ref.shape) == 3:
            return ref.at[which] if rows is None else ref.at[which, rows]
        lanes = pl.ds(pl.multiple_of(which * half, half), half)
        return ref.at[:, lanes] if rows is None else ref.at[rows, lanes]

    sends = []

    def begin(copy):
        copy.start()
        sends.append(copy)
        return copy

    def to_sib(j, block, send, recv):
        return begin(push(wbuf.at[j, block, mine], wbuf.at[j, block, mine], send, recv, "cand", sib))

    def send_a(j):
        return begin(push(part(weights[j], 1 - x, mine), wbuf.at[j, u, mine],
                          a_s.at[j], a_r.at[j], "user", mate))

    def send_b(j):
        return [
            begin(push(part(weights[j], x, mine), wbuf.at[j, u, mine],
                       b_s.at[j, dq - 1], b_r.at[j, dq - 1], "user", above(dq)))
            for dq in range(1, cols)
        ]

    def send_c(j):
        return [
            begin(push(wbuf.at[j, mate, mine], wbuf.at[j, mate, mine],
                       c_s.at[j, dq - 1], c_r.at[j, dq - 1], "user", above(dq)))
            for dq in range(1, cols)
        ]

    rows_half = tokens // 2
    piece = rows_half // chunks
    first = lax.rem(g, 2)

    def piece_rows(which, i):
        return pl.ds(pl.multiple_of(which * rows_half + i * piece, piece), piece)

    def send_n(i):
        return begin(push(states_ref.at[piece_rows(first, i)], part_raw.at[piece_rows(first, i)],
                          n_s.at[i], n_r.at[i], "user", mate))

    def send_z(i):
        return begin(push(part_raw.at[piece_rows(first, i)], part_raw.at[piece_rows(first, i)],
                          z_s.at[i], z_r.at[i], "gen", gen_mate))

    a0, b0 = send_a(0), send_b(0)
    locals_ = []
    for j in range(2):
        copy = pltpu.make_async_copy(part(weights[j], x, None), wbuf.at[j, u], loc.at[j])
        copy.start()
        locals_.append(copy)

    step = 64

    def norm_own(i, _):
        rows = pl.ds(pl.multiple_of(i * step, step), step)
        own_norm[rows] = normalise(states_ref[rows], gain_ref[...])
        return 0

    lax.fori_loop(0, tokens // step, norm_own, 0)
    for copy in locals_:
        copy.wait()

    def own_block(block, start):
        lanes = pl.ds(pl.multiple_of(block * depth, depth), depth)
        for j in range(2):
            term = jnp.dot(own_norm[:, lanes], wbuf[j, block], preferred_element_type=F32)
            acc[j] = term if start else acc[j] + term

    own_block(u, True)

    def below(dq):
        return lax.rem(q + cols - dq, cols) * 2

    sib_a, sib_b, sib_c, c_copies = [], [], [], []
    a0.wait_recv()
    a1 = send_a(1)
    c_copies.append(send_c(0))
    b1 = send_b(1)
    sib_a.append(to_sib(0, mate, sa_s.at[0], sa_r.at[0]))
    for dq in range(1, cols):
        b0[dq - 1].wait_recv()
        sib_b.append(to_sib(0, below(dq) + x, sb_s.at[0, dq - 1], sb_r.at[0, dq - 1]))
    a1.wait_recv()
    n_copies = [send_n(0)]
    if chunks > 1:
        n_copies.append(send_n(1))
    c_copies.append(send_c(1))
    sib_a.append(to_sib(1, mate, sa_s.at[1], sa_r.at[1]))
    for copy in sib_a:
        copy.wait_recv()
    own_block(mate, False)
    z_copies = []

    def pass_on(i):
        n_copies[i].wait_recv()
        z_copies.append(send_z(i))
        if i + 2 < chunks:
            n_copies.append(send_n(i + 2))

    for dq in range(1, cols):
        b1[dq - 1].wait_recv()
        sib_b.append(to_sib(1, below(dq) + x, sb_s.at[1, dq - 1], sb_r.at[1, dq - 1]))
    pass_on(0)
    for copy in sib_b:
        copy.wait_recv()
    for dq in range(1, cols):
        own_block(below(dq) + x, False)
    for j in range(2):
        if j + 1 < chunks:
            pass_on(j + 1)
        for dq in range(1, cols):
            c_copies[j][dq - 1].wait_recv()
            sib_c.append(to_sib(j, below(dq) + 1 - x, sc_s.at[j, dq - 1], sc_r.at[j, dq - 1]))
    for i in range(3, chunks):
        pass_on(i)
    for copy in sib_c:
        copy.wait_recv()
    for dq in range(1, cols):
        own_block(below(dq) + 1 - x, False)

    groups = tokens // STEPS
    out_rows = 2 * piece // STEPS
    pool = pool_matrix(out_rows)

    def pooled(gate, up):
        hidden = (jax.nn.silu(gate) * up).astype(BF16)
        return jnp.dot(pool, hidden, preferred_element_type=F32).astype(BF16)

    def own_out(i, _):
        rows = pl.ds(pl.multiple_of(i * 2 * piece, 2 * piece), 2 * piece)
        at = pl.multiple_of(x * groups + i * out_rows, out_rows)
        ph_ref[pl.ds(at, out_rows)] = pooled(acc[0, rows], acc[1, rows])
        return 0

    lax.fori_loop(0, tokens // (2 * piece), own_out, 0)

    for i in range(chunks):
        part_norm[:piece] = normalise(part_raw[piece_rows(first, i)], gain_ref[...])
        z_copies[i].wait_recv()
        part_norm[piece:] = normalise(part_raw[piece_rows(1 - first, i)], gain_ref[...])
        both = []
        for j in range(2):
            total = None
            for block in range(n_user):
                term = jnp.dot(part_norm[:, block * depth:(block + 1) * depth], wbuf[j, block],
                               preferred_element_type=F32)
                total = term if total is None else total + term
            both.append(total)
        out = pooled(*both)
        small = out_rows // 2
        for k, which in enumerate((first, 1 - first)):
            at = pl.multiple_of(
                (1 - x) * groups + which * (rows_half // STEPS) + i * small, small
            )
            ph_ref[pl.ds(at, small)] = out[k * small:(k + 1) * small]

    for copy in sends:
        copy.wait_send()


def split_columns(weight):
    half = weight.shape[1] // 2
    if half % 128 == 0:
        return weight
    return weight.reshape(weight.shape[0], 2, half).transpose(1, 0, 2)


def head(states, norm_gain, gate_weight, up_weight):
    n_gen, n_user, n_cand = (lax.axis_size(a) for a in ("gen", "user", "cand"))
    tokens, width = states.shape
    depth, half = gate_weight.shape[0], gate_weight.shape[1] // 2
    chunks = 4
    cols = n_user // 2
    vmem = pltpu.VMEM
    dma = pltpu.SemaphoreType.DMA
    many = dma((2, cols - 1))
    anywhere = pl.BlockSpec(memory_space=pl.ANY)
    inside = pl.BlockSpec(memory_space=vmem)
    return pl.pallas_call(
        functools.partial(head_kernel, n_gen, n_user, n_cand, chunks),
        out_shape=jax.ShapeDtypeStruct((2 * tokens // STEPS, half), BF16),
        in_specs=[inside, inside, anywhere, anywhere],
        out_specs=inside,
        scratch_shapes=[
            vmem((2, n_user, depth, half), BF16),
            vmem((tokens, width), BF16),
            vmem((tokens, width), BF16),
            vmem((tokens // chunks, width), BF16),
            vmem((2, tokens, half), F32),
            dma((2,)),
            dma((2,)), dma((2,)), many, many, many, many,
            dma((2,)), dma((2,)), many, many, many, many,
            dma((chunks,)), dma((chunks,)), dma((chunks,)), dma((chunks,)),
        ],
        compiler_params=pltpu.CompilerParams(
            collective_id=1, has_side_effects=True, vmem_limit_bytes=56 * 1024 * 1024
        ),
    )(states, norm_gain.reshape(1, width), split_columns(gate_weight), split_columns(up_weight))


def tail_kernel(
    n_gen, n_user, n_cand, ratio,
    ph_ref, down_ref, proj_ref, ein_ref, enc_ref, cap_ref, out_ref,
    proj, ph_in, e_own, rs_out, rs_in, zr_out, zr_in, cz, call_in, kern,
    tot_out, tot_in, vote_mine, vote_u_in, vote_g_mine, vote_g_in,
    pj_s, pj_r, ph_s, ph_r, rs_s, rs_r, zr_s, zr_r, cz_s, cz_r, ca_s, ca_r,
    tot_s, tot_r, vu_s, vu_r, vg_s, vg_r,
):
    u = lax.axis_index("user")
    g = lax.axis_index("gen")
    c = lax.axis_index("cand")
    sib = lax.rem(c + 1, n_cand)
    groups = ein_ref.shape[0]
    half = ph_ref.shape[1]
    cols = n_user // 2
    q, x = u // 2, lax.rem(u, 2)
    greet((("user", n_user), ("gen", n_gen), ("cand", n_cand)))

    def peer_u(k):
        return lax.rem(u + k, n_user)

    def peer_g(k):
        return lax.rem(g + k, n_gen)

    def ph_copy(dq, dx):
        k = dq * 2 + dx - 1
        peer = lax.rem(q + dq, cols) * 2 + lax.rem(x + dx, 2)
        return push(ph_ref, ph_in.at[u], ph_s.at[k], ph_r.at[k], "user", peer)

    shifts = [(dq, dx) for dq in range(cols) for dx in range(2)][1:]
    for shift in shifts:
        ph_copy(*shift).start()
    proj_rows = proj_ref.shape[0]
    own_rows = pl.ds(pl.multiple_of(c * proj_rows, proj_rows), proj_rows)
    pj_copy = push(proj_ref, proj.at[own_rows], pj_s.at[0], pj_r.at[0], "cand", sib)
    pj_copy.start()
    proj[own_rows] = proj_ref[...]
    ph_in[u] = ph_ref[...]
    pj_copy.wait_recv()

    def rs_copy(dq, dx):
        k = dq * 2 + dx - 1
        peer = lax.rem(q + cols - dq, cols) * 2 + lax.rem(x + dx, 2)
        return push(rs_out.at[k], rs_in.at[k], rs_s.at[k], rs_r.at[k], "user", peer)

    def embed(dq):
        there = lax.rem(q + cols - dq, cols) * 2
        mixed = jnp.dot(ph_in[there], down_ref[:half], preferred_element_type=F32)
        mixed += jnp.dot(ph_in[there + 1], down_ref[half:], preferred_element_type=F32)
        full = jnp.dot(mixed.astype(BF16), proj[...], preferred_element_type=F32)
        near = jnp.where(x == 0, full[:groups], full[groups:])
        far = jnp.where(x == 0, full[groups:], full[:groups])
        return near, far

    ph_copy(0, 1).wait_recv()
    near, far = embed(0)
    rs_out[0] = far.astype(BF16)
    rs_copy(0, 1).start()
    e_own[...] = near + ein_ref[...]

    def step(dq, _):
        ph_copy(dq, 0).wait_recv()
        ph_copy(dq, 1).wait_recv()
        near, far = embed(dq)
        rs_out[dq * 2 - 1] = near.astype(BF16)
        rs_copy(dq, 0).start()
        rs_out[dq * 2] = far.astype(BF16)
        rs_copy(dq, 1).start()
        return 0

    lax.fori_loop(1, cols, step, 0)
    total = e_own[...]
    for dq, dx in shifts:
        rs_copy(dq, dx).wait_recv()
        total = total + rs_in[dq * 2 + dx - 1].astype(F32)

    share = groups // n_gen
    zr_out[...] = total.reshape(n_gen, share, total.shape[1])
    own_sum = zr_out[g]
    zr_copy = []
    for k in range(1, n_gen):
        cz[k] = zr_out[peer_g(k)].astype(BF16)
        copy = push(cz.at[k], zr_in.at[k - 1], zr_s.at[k - 1], zr_r.at[k - 1], "gen", peer_g(k))
        copy.start()
        zr_copy.append(copy)
    for k in range(1, n_gen):
        zr_copy[k - 1].wait_recv()
        own_sum = own_sum + zr_in[k - 1].astype(F32)
    own_sum = own_sum * (1.0 / STEPS)
    cz[0] = unit_rows(own_sum)

    cg_copy = []
    for k in range(1, n_gen):
        copy = push(cz.at[0], call_in.at[0, pl.ds(pl.multiple_of(g * share, share), share)],
                    cz_s.at[k - 1], cz_r.at[k - 1], "gen", peer_g(k))
        copy.start()
        cg_copy.append(copy)
    call_in[0, pl.ds(pl.multiple_of(g * share, share), share)] = cz[0]
    for copy in cg_copy:
        copy.wait_recv()
    ca_copy = []
    for k in range(1, n_user):
        copy = push(call_in.at[0], call_in.at[k], ca_s.at[k - 1], ca_r.at[k - 1], "user", peer_u(k))
        copy.start()
        ca_copy.append(copy)

    def score(k):
        scores = lax.dot_general(
            enc_ref[...], call_in[k], (((1,), (1,)), ((), ())), preferred_element_type=F32
        )
        value = jnp.exp(scores * 60.0)
        kern[k] = value
        return jnp.sum(value, axis=1, keepdims=True)

    totals = score(0)
    for k in range(1, n_user):
        ca_copy[k - 1].wait_recv()
        totals = totals + score(k)
    tot_out[...] = jnp.broadcast_to(totals, tot_out.shape)
    tot_copy = push(tot_out, tot_in, tot_s.at[0], tot_r.at[0], "cand", sib)
    tot_copy.start()
    tot_copy.wait_recv()
    totals = totals + tot_in[:, :1]
    weight = cap_ref[...] / totals * ratio
    for k in range(n_user):
        part = jnp.sum(kern[k] * weight, axis=0, keepdims=True)
        vote_mine[lax.rem(u + n_user - k, n_user)] = jnp.broadcast_to(part, vote_mine.shape[1:])

    vu_copy = []
    for k in range(1, n_user):
        copy = push(vote_mine, vote_u_in.at[k - 1], vu_s.at[k - 1], vu_r.at[k - 1], "user", peer_u(k))
        copy.start()
        vu_copy.append(copy)
    votes = vote_mine[...]
    for k in range(1, n_user):
        vu_copy[k - 1].wait_recv()
        votes = votes + vote_u_in[k - 1]
    vote_g_mine[...] = votes
    vg_copy = []
    for k in range(1, n_gen):
        copy = push(vote_g_mine, vote_g_in.at[k - 1], vg_s.at[k - 1], vg_r.at[k - 1], "gen", peer_g(k))
        copy.start()
        vg_copy.append(copy)
    for k in range(1, n_gen):
        vg_copy[k - 1].wait_recv()
        votes = votes + vote_g_in[k - 1]
    out_ref[...] = votes[:, :1, :]

    for copy in [pj_copy] + zr_copy + cg_copy + ca_copy + [tot_copy] + vu_copy + vg_copy:
        copy.wait_send()
    for shift in shifts:
        ph_copy(*shift).wait_send()
        rs_copy(*shift).wait_send()


def tail(hidden_sum, down_weight, proj_user, e_in, encoded, row_cap, ratio):
    n_gen, n_user, n_cand = (lax.axis_size(a) for a in ("gen", "user", "cand"))
    groups, emb = e_in.shape
    rows = encoded.shape[0]
    share = groups // n_gen
    vmem = pltpu.VMEM
    dma = pltpu.SemaphoreType.DMA
    nu, ng = n_user - 1, n_gen - 1
    return pl.pallas_call(
        functools.partial(tail_kernel, n_gen, n_user, n_cand, ratio),
        out_shape=jax.ShapeDtypeStruct((n_user, 1, groups), F32),
        in_specs=[pl.BlockSpec(memory_space=vmem)] * 6,
        out_specs=pl.BlockSpec(memory_space=vmem),
        scratch_shapes=[
            vmem((n_cand * proj_user.shape[0], emb), BF16),
            vmem((n_user, *hidden_sum.shape), BF16),
            vmem((groups, emb), F32),
            vmem((nu, groups, emb), BF16),
            vmem((nu, groups, emb), BF16),
            vmem((n_gen, share, emb), F32),
            vmem((ng, share, emb), BF16),
            vmem((n_gen, share, emb), BF16),
            vmem((n_user, groups, emb), BF16),
            vmem((n_user, rows, groups), F32),
            vmem((rows, 128), F32),
            vmem((rows, 128), F32),
            vmem((n_user, 8, groups), F32),
            vmem((nu, n_user, 8, groups), F32),
            vmem((n_user, 8, groups), F32),
            vmem((ng, n_user, 8, groups), F32),
            dma((1,)), dma((1,)),
            dma((nu,)), dma((nu,)),
            dma((nu,)), dma((nu,)),
            dma((ng,)), dma((ng,)),
            dma((ng,)), dma((ng,)),
            dma((nu,)), dma((nu,)),
            dma((1,)), dma((1,)),
            dma((nu,)), dma((nu,)),
            dma((ng,)), dma((ng,)),
        ],
        compiler_params=pltpu.CompilerParams(
            collective_id=0, has_side_effects=True, vmem_limit_bytes=56 * 1024 * 1024
        ),
    )(hidden_sum, down_weight, proj_user, e_in, encoded, row_cap)


def proj_of_user(proj_weight):
    n_gen, n_user = lax.axis_size("gen"), lax.axis_size("user")
    per = n_user // n_gen
    rows = proj_weight.shape[0] // per
    part = rows // lax.axis_size("cand")
    slot = lax.rem(lax.axis_index("user"), per)
    start = slot * rows + lax.axis_index("cand") * part
    piece = lax.dynamic_slice_in_dim(proj_weight, start, part, 0)
    pairs = [
        (a * n_user + b, (b // per) * n_user + a * per + b % per)
        for a in range(n_gen) for b in range(n_user)
    ]
    return lax.ppermute(piece, ("gen", "user"), pairs)


def shards(
    states,
    norm_gain,
    gate_weight,
    up_weight,
    down_weight,
    proj_weight,
    private_rows,
    enc_weight,
    user_ids,
):
    tok_rows = states.shape[0]
    groups = tok_rows // STEPS
    hidden_sum = head(states, norm_gain, gate_weight, up_weight)
    proj_user = proj_of_user(proj_weight)
    slab_width = proj_weight.shape[0]
    own_cols = lax.dynamic_slice_in_dim(states, lax.axis_index("gen") * slab_width, slab_width, 1)
    pooled_in = jnp.dot(pool_matrix(groups), own_cols, preferred_element_type=F32).astype(BF16)
    e_in = jnp.dot(pooled_in, proj_weight, preferred_element_type=F32)
    encoded = unit_rows(jnp.dot(private_rows, enc_weight, preferred_element_type=F32))
    member = (user_ids[:, None] == jnp.arange(USERS_DEV, dtype=jnp.int32)[None, :]).astype(F32)
    counts = jnp.sum(member, axis=0)
    limit = jnp.minimum(1.0, CAP / jnp.maximum(counts, 1.0))
    row_cap = jnp.sum(member * limit[None, :], axis=1, keepdims=True)
    row_total = private_rows.shape[0] * lax.axis_size("gen") * lax.axis_size("user")
    cand_total = groups * lax.axis_size("user") * lax.axis_size("cand")
    return tail(
        hidden_sum, down_weight, proj_user, e_in, encoded, row_cap, cand_total / row_total
    )


def solution(mesh):
    return jax.shard_map(
        shards,
        mesh=mesh,
        in_specs=(
            P(("user", "cand"), None),
            P(),
            P("user", "gen"),
            P("user", "gen"),
            P("gen", "user"),
            P("gen", None),
            P(("gen", "user"), None),
            P(),
            P(("gen", "user")),
        ),
        out_specs=P(None, "cand", None),
        check_vma=False,
    )
```

```python
import functools

import jax
import jax.numpy as jnp
from jax import lax
from jax.experimental import pallas as pl
from jax.experimental.pallas import tpu as pltpu
from jax.sharding import PartitionSpec as P

STEPS = 4
CAP = 8
USERS_DEV = 32
F32 = jnp.float32
BF16 = jnp.bfloat16
MESH = pl.DeviceIdType.MESH


def unit_rows(matrix):
    return (matrix * lax.rsqrt(jnp.sum(matrix * matrix, axis=1, keepdims=True) + 1e-06)).astype(BF16)


def pool_matrix(groups):
    rows = lax.broadcasted_iota(jnp.int32, (groups, groups * STEPS), 0)
    cols = lax.broadcasted_iota(jnp.int32, (groups, groups * STEPS), 1)
    return (cols // STEPS == rows).astype(BF16)


def greet(sizes):
    barrier = pltpu.get_barrier_semaphore()
    count = 0
    for axis, size in sizes:
        me = lax.axis_index(axis)
        for k in range(1, size):
            pl.semaphore_signal(
                barrier, inc=1, device_id={axis: lax.rem(me + k, size)}, device_id_type=MESH
            )
            count += 1
    pl.semaphore_wait(barrier, count)


def push(src, dst, send, recv, axis, peer):
    return pltpu.make_async_remote_copy(
        src_ref=src, dst_ref=dst, send_sem=send, recv_sem=recv,
        device_id={axis: peer}, device_id_type=MESH,
    )


def normalise(block, gain):
    values = block.astype(F32)
    scale = lax.rsqrt(jnp.mean(values * values, axis=1, keepdims=True) + 1e-05)
    return (values * scale * gain).astype(BF16)


def head_kernel(
    n_gen, n_user, n_cand, chunks,
    states_ref, gain_ref, gate_ref, up_ref, proj_ref, ph_ref, proj_out,
    wbuf, norm, part_raw, acc,
    loc, a_s, a_r, b_s, b_r, c_s, c_r, sa_s, sa_r, sb_s, sb_r, sc_s, sc_r, n_s, n_r, z_s, z_r,
    p_s, p_r,
):
    u = lax.axis_index("user")
    g = lax.axis_index("gen")
    c = lax.axis_index("cand")
    cols = n_user // 2
    q, x = u // 2, lax.rem(u, 2)
    mate = q * 2 + 1 - x
    gen_mate = (g // 2) * 2 + 1 - lax.rem(g, 2)
    sib = lax.rem(c + 1, n_cand)
    tokens, width = states_ref.shape
    depth, half = wbuf.shape[2], wbuf.shape[3]
    share = depth // n_cand
    mine = pl.ds(pl.multiple_of(c * share, share), share)
    weights = (gate_ref, up_ref)
    others = range(1, cols)

    def above(dq):
        return lax.rem(q + dq, cols) * 2 + x

    def below(dq):
        return lax.rem(q + cols - dq, cols) * 2

    greet((("user", n_user), ("gen", n_gen), ("cand", n_cand)))

    def part(ref, which, rows):
        if len(ref.shape) == 3:
            return ref.at[which] if rows is None else ref.at[which, rows]
        lanes = pl.ds(pl.multiple_of(which * half, half), half)
        return ref.at[:, lanes] if rows is None else ref.at[rows, lanes]

    sends = []

    def begin(copy):
        copy.start()
        sends.append(copy)
        return copy

    def to_sib(j, block, send, recv):
        return begin(push(wbuf.at[j, block, mine], wbuf.at[j, block, mine], send, recv, "cand", sib))

    def send_a(j):
        return begin(push(part(weights[j], 1 - x, mine), wbuf.at[j, u, mine],
                          a_s.at[j], a_r.at[j], "user", mate))

    def send_b(j):
        return [
            begin(push(part(weights[j], x, mine), wbuf.at[j, u, mine],
                       b_s.at[j, dq - 1], b_r.at[j, dq - 1], "user", above(dq)))
            for dq in others
        ]

    def send_c(j):
        return [
            begin(push(wbuf.at[j, mate, mine], wbuf.at[j, mate, mine],
                       c_s.at[j, dq - 1], c_r.at[j, dq - 1], "user", above(dq)))
            for dq in others
        ]

    rows_half = tokens // 2
    piece = rows_half // chunks
    first = lax.rem(g, 2)

    def piece_rows(which, i):
        return pl.ds(pl.multiple_of(which * rows_half + i * piece, piece), piece)

    def send_n(i):
        return begin(push(states_ref.at[piece_rows(first, i)], part_raw.at[piece_rows(first, i)],
                          n_s.at[i], n_r.at[i], "user", mate))

    def send_z(i):
        return begin(push(part_raw.at[piece_rows(first, i)], part_raw.at[piece_rows(first, i)],
                          z_s.at[i], z_r.at[i], "gen", gen_mate))

    per = n_user // n_gen
    owner = u // per
    far = jnp.where(g > owner, g - owner, owner - g)
    p_rows = proj_out.shape[0]
    p_at = pl.ds(pl.multiple_of(lax.rem(u, per) * (n_cand * p_rows) + c * p_rows, p_rows), p_rows)

    def proj_up():
        return push(proj_out, proj_out, p_s.at[0], p_r.at[0], "gen", lax.rem(g + 1, n_gen))

    def proj_down():
        return push(proj_out, proj_out, p_s.at[1], p_r.at[0], "gen", lax.rem(g + n_gen - 1, n_gen))

    goes_up = jnp.logical_and(g >= owner, g < n_gen - 1)
    goes_down = jnp.logical_and(g <= owner, g > 0)

    def proj_pass():
        @pl.when(goes_up)
        def _():
            proj_up().start()

        @pl.when(goes_down)
        def _():
            proj_down().start()

    def proj_step(k):
        @pl.when(far == k)
        def _():
            proj_up().wait_recv()
            proj_pass()

    a0, b0 = send_a(0), send_b(0)
    locals_ = []
    for j in range(2):
        copy = pltpu.make_async_copy(part(weights[j], x, None), wbuf.at[j, u], loc.at[j])
        copy.start()
        locals_.append(copy)

    @pl.when(far == 0)
    def _():
        copy = pltpu.make_async_copy(proj_ref.at[p_at], proj_out, loc.at[2])
        copy.start()
        copy.wait()
        proj_pass()

    step = 64

    def norm_own(i, _):
        rows = pl.ds(pl.multiple_of(i * step, step), step)
        norm[rows] = normalise(states_ref[rows], gain_ref[...])
        return 0

    def norm_part(i):
        n_at = tokens + 2 * i * piece
        norm[n_at:n_at + piece] = normalise(part_raw[piece_rows(first, i)], gain_ref[...])
        z_copies[i].wait_recv()
        norm[n_at + piece:n_at + 2 * piece] = normalise(
            part_raw[piece_rows(1 - first, i)], gain_ref[...]
        )

    def dots(j, block, low, high, start=False):
        lanes = pl.ds(pl.multiple_of(block * depth, depth), depth)
        term = jnp.dot(norm[low:high, lanes], wbuf[j, block], preferred_element_type=F32)
        acc[j, low:high] = term if start else acc[j, low:high] + term

    lax.fori_loop(0, tokens // step, norm_own, 0)
    for copy in locals_:
        copy.wait()
    for j in range(2):
        dots(j, u, 0, tokens, True)

    early = tokens + (chunks // 2) * 2 * piece
    sib_b, n_copies, z_copies = [], [], []

    def pass_n(i):
        n_copies[i].wait_recv()
        z_copies.append(send_z(i))

    a0.wait_recv()
    n_copies += [send_n(0), send_n(1)]
    c0 = send_c(0)
    b1 = send_b(1)
    sib_a0 = to_sib(0, mate, sa_s.at[0], sa_r.at[0])
    for dq in others:
        b0[dq - 1].wait_recv()
        sib_b.append(to_sib(0, below(dq) + x, sb_s.at[0, dq - 1], sb_r.at[0, dq - 1]))
    pass_n(0)
    a1 = send_a(1)
    pass_n(1)
    n_copies.append(send_n(2))
    proj_step(1)
    sib_a0.wait_recv()
    dots(0, mate, 0, tokens)
    for dq in others:
        b1[dq - 1].wait_recv()
        sib_b.append(to_sib(1, below(dq) + x, sb_s.at[1, dq - 1], sb_r.at[1, dq - 1]))
    a1.wait_recv()
    n_copies.append(send_n(3))
    c1 = send_c(1)
    sib_a1 = to_sib(1, mate, sa_s.at[1], sa_r.at[1])
    proj_step(2)
    for copy in sib_b:
        copy.wait_recv()
    for dq in others:
        for j in range(2):
            dots(j, below(dq) + x, 0, tokens)
    pass_n(2)
    for i in range(chunks // 2):
        norm_part(i)
    for j in range(2):
        dots(j, u, tokens, early, True)
    sib_c = []
    for dq in others:
        c0[dq - 1].wait_recv()
        sib_c.append(to_sib(0, below(dq) + 1 - x, sc_s.at[0, dq - 1], sc_r.at[0, dq - 1]))
    dots(0, mate, tokens, early)
    sib_a1.wait_recv()
    dots(1, mate, 0, early)
    pass_n(3)
    for k in range(3, n_gen):
        proj_step(k)
    for dq in others:
        for j in range(2):
            dots(j, below(dq) + x, tokens, early)
    for copy in sib_c:
        copy.wait_recv()
    for dq in others:
        dots(0, below(dq) + 1 - x, 0, early)
    norm_part(2)
    sib_c = []
    for dq in others:
        c1[dq - 1].wait_recv()
        sib_c.append(to_sib(1, below(dq) + 1 - x, sc_s.at[1, dq - 1], sc_r.at[1, dq - 1]))
    for copy in sib_c:
        copy.wait_recv()
    for dq in others:
        dots(1, below(dq) + 1 - x, 0, early)

    groups = tokens // STEPS
    out_rows = 2 * piece // STEPS
    small = out_rows // 2
    pool = pool_matrix(out_rows)

    def pooled(gate, up):
        hidden = (jax.nn.silu(gate) * up).astype(BF16)
        return jnp.dot(pool, hidden, preferred_element_type=F32).astype(BF16)

    def own_out(i, _):
        rows = pl.ds(pl.multiple_of(i * 2 * piece, 2 * piece), 2 * piece)
        at = pl.multiple_of(x * groups + i * out_rows, out_rows)
        ph_ref[pl.ds(at, out_rows)] = pooled(acc[0, rows], acc[1, rows])
        return 0

    def part_out(i, out):
        for k, which in enumerate((first, 1 - first)):
            at = pl.multiple_of(
                (1 - x) * groups + which * (rows_half // STEPS) + i * small, small
            )
            ph_ref[pl.ds(at, small)] = out[k * small:(k + 1) * small]

    lax.fori_loop(0, tokens // (2 * piece), own_out, 0)
    for i in range(chunks // 2):
        rows = slice(tokens + 2 * i * piece, tokens + 2 * (i + 1) * piece)
        part_out(i, pooled(acc[0, rows], acc[1, rows]))
    norm_part(3)
    both = []
    for j in range(2):
        total = None
        for block in range(n_user):
            term = jnp.dot(norm[early:, block * depth:(block + 1) * depth], wbuf[j, block],
                           preferred_element_type=F32)
            total = term if total is None else total + term
        both.append(total)
    for i in range(chunks // 2, chunks):
        rows = slice(2 * i * piece + tokens - early, 2 * (i + 1) * piece + tokens - early)
        part_out(i, pooled(both[0][rows], both[1][rows]))

    for copy in sends:
        copy.wait_send()

    @pl.when(goes_up)
    def _():
        proj_up().wait_send()

    @pl.when(goes_down)
    def _():
        proj_down().wait_send()


def split_columns(weight):
    half = weight.shape[1] // 2
    if half % 128 == 0:
        return weight
    return weight.reshape(weight.shape[0], 2, half).transpose(1, 0, 2)


def head(states, norm_gain, gate_weight, up_weight, proj_weight):
    n_gen, n_user, n_cand = (lax.axis_size(a) for a in ("gen", "user", "cand"))
    tokens, width = states.shape
    depth, half = gate_weight.shape[0], gate_weight.shape[1] // 2
    chunks = 4
    proj_rows = proj_weight.shape[0] * n_gen // (n_user * n_cand)
    cols = n_user // 2
    vmem = pltpu.VMEM
    dma = pltpu.SemaphoreType.DMA
    many = dma((2, cols - 1))
    anywhere = pl.BlockSpec(memory_space=pl.ANY)
    inside = pl.BlockSpec(memory_space=vmem)
    return pl.pallas_call(
        functools.partial(head_kernel, n_gen, n_user, n_cand, chunks),
        out_shape=(
            jax.ShapeDtypeStruct((2 * tokens // STEPS, half), BF16),
            jax.ShapeDtypeStruct((proj_rows, proj_weight.shape[1]), BF16),
        ),
        in_specs=[inside, inside, anywhere, anywhere, anywhere],
        out_specs=(inside, inside),
        scratch_shapes=[
            vmem((2, n_user, depth, half), BF16),
            vmem((2 * tokens, width), BF16),
            vmem((tokens, width), BF16),
            vmem((2, tokens + tokens // 2, half), F32),
            dma((3,)),
            dma((2,)), dma((2,)), many, many, many, many,
            dma((2,)), dma((2,)), many, many, many, many,
            dma((chunks,)), dma((chunks,)), dma((chunks,)), dma((chunks,)),
            dma((2,)), dma((1,)),
        ],
        compiler_params=pltpu.CompilerParams(
            collective_id=1, has_side_effects=True, vmem_limit_bytes=56 * 1024 * 1024
        ),
    )(states, norm_gain.reshape(1, width), split_columns(gate_weight), split_columns(up_weight),
      proj_weight)


def tail_kernel(
    n_gen, n_user, n_cand, ratio,
    ph_ref, down_ref, proj_ref, ein_ref, enc_ref, cap_ref, out_ref,
    proj, ph_in, e_own, rs_out, rs_in, zr_out, zr_in, cz, call_in, kern,
    tot_out, tot_in, vote_mine, vote_u_in, vote_g_mine, vote_g_in,
    pj_s, pj_r, ph_s, ph_r, rs_s, rs_r, zr_s, zr_r, cz_s, cz_r, ca_s, ca_r,
    tot_s, tot_r, vu_s, vu_r, vg_s, vg_r,
):
    u = lax.axis_index("user")
    g = lax.axis_index("gen")
    c = lax.axis_index("cand")
    sib = lax.rem(c + 1, n_cand)
    groups = ein_ref.shape[0]
    half = ph_ref.shape[1]
    cols = n_user // 2
    q, x = u // 2, lax.rem(u, 2)
    greet((("user", n_user), ("gen", n_gen), ("cand", n_cand)))

    def peer_u(k):
        return lax.rem(u + k, n_user)

    def peer_g(k):
        return lax.rem(g + k, n_gen)

    def ph_copy(dq, dx):
        k = dq * 2 + dx - 1
        peer = lax.rem(q + dq, cols) * 2 + lax.rem(x + dx, 2)
        return push(ph_ref, ph_in.at[u], ph_s.at[k], ph_r.at[k], "user", peer)

    shifts = [(dq, dx) for dq in range(cols) for dx in range(2)][1:]
    for shift in shifts:
        ph_copy(*shift).start()
    proj_rows = proj_ref.shape[0]
    own_rows = pl.ds(pl.multiple_of(c * proj_rows, proj_rows), proj_rows)
    pj_copy = push(proj_ref, proj.at[own_rows], pj_s.at[0], pj_r.at[0], "cand", sib)
    pj_copy.start()
    proj[own_rows] = proj_ref[...]
    ph_in[u] = ph_ref[...]
    pj_copy.wait_recv()

    def rs_copy(dq, dx):
        k = dq * 2 + dx - 1
        peer = lax.rem(q + cols - dq, cols) * 2 + lax.rem(x + dx, 2)
        return push(rs_out.at[k], rs_in.at[k], rs_s.at[k], rs_r.at[k], "user", peer)

    def embed(dq):
        there = lax.rem(q + cols - dq, cols) * 2
        mixed = jnp.dot(ph_in[there], down_ref[:half], preferred_element_type=F32)
        mixed += jnp.dot(ph_in[there + 1], down_ref[half:], preferred_element_type=F32)
        full = jnp.dot(mixed.astype(BF16), proj[...], preferred_element_type=F32)
        near = jnp.where(x == 0, full[:groups], full[groups:])
        far = jnp.where(x == 0, full[groups:], full[:groups])
        return near, far

    ph_copy(0, 1).wait_recv()
    near, far = embed(0)
    rs_out[0] = far.astype(BF16)
    rs_copy(0, 1).start()
    e_own[...] = near + ein_ref[...]

    def step(dq, _):
        ph_copy(dq, 0).wait_recv()
        ph_copy(dq, 1).wait_recv()
        near, far = embed(dq)
        rs_out[dq * 2 - 1] = near.astype(BF16)
        rs_copy(dq, 0).start()
        rs_out[dq * 2] = far.astype(BF16)
        rs_copy(dq, 1).start()
        return 0

    lax.fori_loop(1, cols, step, 0)
    total = e_own[...]
    for dq, dx in shifts:
        rs_copy(dq, dx).wait_recv()
        total = total + rs_in[dq * 2 + dx - 1].astype(F32)

    share = groups // n_gen
    zr_out[...] = total.reshape(n_gen, share, total.shape[1])
    own_sum = zr_out[g]
    zr_copy = []
    for k in range(1, n_gen):
        cz[k] = zr_out[peer_g(k)].astype(BF16)
        copy = push(cz.at[k], zr_in.at[k - 1], zr_s.at[k - 1], zr_r.at[k - 1], "gen", peer_g(k))
        copy.start()
        zr_copy.append(copy)
    for k in range(1, n_gen):
        zr_copy[k - 1].wait_recv()
        own_sum = own_sum + zr_in[k - 1].astype(F32)
    own_sum = own_sum * (1.0 / STEPS)
    cz[0] = unit_rows(own_sum)

    cg_copy = []
    for k in range(1, n_gen):
        copy = push(cz.at[0], call_in.at[0, pl.ds(pl.multiple_of(g * share, share), share)],
                    cz_s.at[k - 1], cz_r.at[k - 1], "gen", peer_g(k))
        copy.start()
        cg_copy.append(copy)
    call_in[0, pl.ds(pl.multiple_of(g * share, share), share)] = cz[0]
    for copy in cg_copy:
        copy.wait_recv()
    ca_copy = []
    for k in range(1, n_user):
        copy = push(call_in.at[0], call_in.at[k], ca_s.at[k - 1], ca_r.at[k - 1], "user", peer_u(k))
        copy.start()
        ca_copy.append(copy)

    def score(k):
        scores = lax.dot_general(
            enc_ref[...], call_in[k], (((1,), (1,)), ((), ())), preferred_element_type=F32
        )
        value = jnp.exp(scores * 60.0)
        kern[k] = value
        return jnp.sum(value, axis=1, keepdims=True)

    totals = score(0)
    for k in range(1, n_user):
        ca_copy[k - 1].wait_recv()
        totals = totals + score(k)
    tot_out[...] = jnp.broadcast_to(totals, tot_out.shape)
    tot_copy = push(tot_out, tot_in, tot_s.at[0], tot_r.at[0], "cand", sib)
    tot_copy.start()
    tot_copy.wait_recv()
    totals = totals + tot_in[:, :1]
    weight = cap_ref[...] / totals * ratio
    for k in range(n_user):
        part = jnp.sum(kern[k] * weight, axis=0, keepdims=True)
        vote_mine[lax.rem(u + n_user - k, n_user)] = jnp.broadcast_to(part, vote_mine.shape[1:])

    vu_copy = []
    for k in range(1, n_user):
        copy = push(vote_mine, vote_u_in.at[k - 1], vu_s.at[k - 1], vu_r.at[k - 1], "user", peer_u(k))
        copy.start()
        vu_copy.append(copy)
    votes = vote_mine[...]
    for k in range(1, n_user):
        vu_copy[k - 1].wait_recv()
        votes = votes + vote_u_in[k - 1]
    vote_g_mine[...] = votes
    vg_copy = []
    for k in range(1, n_gen):
        copy = push(vote_g_mine, vote_g_in.at[k - 1], vg_s.at[k - 1], vg_r.at[k - 1], "gen", peer_g(k))
        copy.start()
        vg_copy.append(copy)
    for k in range(1, n_gen):
        vg_copy[k - 1].wait_recv()
        votes = votes + vote_g_in[k - 1]
    out_ref[...] = votes[:, :1, :]

    for copy in [pj_copy] + zr_copy + cg_copy + ca_copy + [tot_copy] + vu_copy + vg_copy:
        copy.wait_send()
    for shift in shifts:
        ph_copy(*shift).wait_send()
        rs_copy(*shift).wait_send()


def tail(hidden_sum, down_weight, proj_user, e_in, encoded, row_cap, ratio):
    n_gen, n_user, n_cand = (lax.axis_size(a) for a in ("gen", "user", "cand"))
    groups, emb = e_in.shape
    rows = encoded.shape[0]
    share = groups // n_gen
    vmem = pltpu.VMEM
    dma = pltpu.SemaphoreType.DMA
    nu, ng = n_user - 1, n_gen - 1
    return pl.pallas_call(
        functools.partial(tail_kernel, n_gen, n_user, n_cand, ratio),
        out_shape=jax.ShapeDtypeStruct((n_user, 1, groups), F32),
        in_specs=[pl.BlockSpec(memory_space=vmem)] * 6,
        out_specs=pl.BlockSpec(memory_space=vmem),
        scratch_shapes=[
            vmem((n_cand * proj_user.shape[0], emb), BF16),
            vmem((n_user, *hidden_sum.shape), BF16),
            vmem((groups, emb), F32),
            vmem((nu, groups, emb), BF16),
            vmem((nu, groups, emb), BF16),
            vmem((n_gen, share, emb), F32),
            vmem((ng, share, emb), BF16),
            vmem((n_gen, share, emb), BF16),
            vmem((n_user, groups, emb), BF16),
            vmem((n_user, rows, groups), F32),
            vmem((rows, 128), F32),
            vmem((rows, 128), F32),
            vmem((n_user, 8, groups), F32),
            vmem((nu, n_user, 8, groups), F32),
            vmem((n_user, 8, groups), F32),
            vmem((ng, n_user, 8, groups), F32),
            dma((1,)), dma((1,)),
            dma((nu,)), dma((nu,)),
            dma((nu,)), dma((nu,)),
            dma((ng,)), dma((ng,)),
            dma((ng,)), dma((ng,)),
            dma((nu,)), dma((nu,)),
            dma((1,)), dma((1,)),
            dma((nu,)), dma((nu,)),
            dma((ng,)), dma((ng,)),
        ],
        compiler_params=pltpu.CompilerParams(
            collective_id=0, has_side_effects=True, vmem_limit_bytes=56 * 1024 * 1024
        ),
    )(hidden_sum, down_weight, proj_user, e_in, encoded, row_cap)


def shards(
    states,
    norm_gain,
    gate_weight,
    up_weight,
    down_weight,
    proj_weight,
    private_rows,
    enc_weight,
    user_ids,
):
    tok_rows = states.shape[0]
    groups = tok_rows // STEPS
    hidden_sum, proj_user = head(states, norm_gain, gate_weight, up_weight, proj_weight)
    slab_width = proj_weight.shape[0]
    own_cols = lax.dynamic_slice_in_dim(states, lax.axis_index("gen") * slab_width, slab_width, 1)
    pooled_in = jnp.dot(pool_matrix(groups), own_cols, preferred_element_type=F32).astype(BF16)
    e_in = jnp.dot(pooled_in, proj_weight, preferred_element_type=F32)
    encoded = unit_rows(jnp.dot(private_rows, enc_weight, preferred_element_type=F32))
    member = (user_ids[:, None] == jnp.arange(USERS_DEV, dtype=jnp.int32)[None, :]).astype(F32)
    counts = jnp.sum(member, axis=0)
    limit = jnp.minimum(1.0, CAP / jnp.maximum(counts, 1.0))
    row_cap = jnp.sum(member * limit[None, :], axis=1, keepdims=True)
    row_total = private_rows.shape[0] * lax.axis_size("gen") * lax.axis_size("user")
    cand_total = groups * lax.axis_size("user") * lax.axis_size("cand")
    return tail(
        hidden_sum, down_weight, proj_user, e_in, encoded, row_cap, cand_total / row_total
    )


def solution(mesh):
    return jax.shard_map(
        shards,
        mesh=mesh,
        in_specs=(
            P(("user", "cand"), None),
            P(),
            P("user", "gen"),
            P("user", "gen"),
            P("gen", "user"),
            P("gen", None),
            P(("gen", "user"), None),
            P(),
            P(("gen", "user")),
        ),
        out_specs=P(None, "cand", None),
        check_vma=False,
    )
```

```python
import functools

import jax
import jax.numpy as jnp
from jax import lax
from jax.experimental import pallas as pl
from jax.experimental.pallas import tpu as pltpu
from jax.sharding import PartitionSpec as P

STEPS = 4
CAP = 8
TAIL_BUFFERS = 13
F32 = jnp.float32
BF16 = jnp.bfloat16
MESH = pl.DeviceIdType.MESH


def unit_rows(matrix):
    return (matrix * lax.rsqrt(jnp.sum(matrix * matrix, axis=1, keepdims=True) + 1e-06)).astype(BF16)


def pool_matrix(groups):
    rows = lax.broadcasted_iota(jnp.int32, (groups, groups * STEPS), 0)
    cols = lax.broadcasted_iota(jnp.int32, (groups, groups * STEPS), 1)
    return (cols // STEPS == rows).astype(BF16)


def greet(sizes):
    barrier = pltpu.get_barrier_semaphore()
    count = 0
    for axis, size in sizes:
        me = lax.axis_index(axis)
        for k in range(1, size):
            pl.semaphore_signal(
                barrier, inc=1, device_id={axis: lax.rem(me + k, size)}, device_id_type=MESH
            )
            count += 1
    pl.semaphore_wait(barrier, count)


def push(src, dst, send, recv, axis, peer):
    return pltpu.make_async_remote_copy(
        src_ref=src, dst_ref=dst, send_sem=send, recv_sem=recv,
        device_id={axis: peer}, device_id_type=MESH,
    )


def normalise(block, gain):
    values = block.astype(F32)
    scale = lax.rsqrt(jnp.mean(values * values, axis=1, keepdims=True) + 1e-05)
    return (values * scale * gain).astype(BF16)


def head_part(
    n_gen, n_user, n_cand, chunks,
    states_ref, gain_ref, gate_ref, up_ref, proj_ref, down_ref, rows_ref, encw_ref,
    ph_in, proj, e_own, down, encoded,
    wbuf, norm, part_raw, acc,
    loc, a_s, a_r, b_s, b_r, c_s, c_r, sa_s, sa_r, sb_s, sb_r, sc_s, sc_r, n_s, n_r, z_s, z_r,
    p_s, p_r, pj_s, pj_r, ph_s, ph_r,
):
    u = lax.axis_index("user")
    g = lax.axis_index("gen")
    c = lax.axis_index("cand")
    cols = n_user // 2
    q, x = u // 2, lax.rem(u, 2)
    mate = q * 2 + 1 - x
    gen_mate = (g // 2) * 2 + 1 - lax.rem(g, 2)
    sib = lax.rem(c + 1, n_cand)
    tokens, width = states_ref.shape
    depth, half = wbuf.shape[2], wbuf.shape[3]
    share = depth // n_cand
    mine = pl.ds(pl.multiple_of(c * share, share), share)
    weights = (gate_ref, up_ref)
    others = range(1, cols)

    def above(dq):
        return lax.rem(q + dq, cols) * 2 + x

    def below(dq):
        return lax.rem(q + cols - dq, cols) * 2

    greet((("user", n_user), ("gen", n_gen), ("cand", n_cand)))

    def part(ref, which, rows):
        if len(ref.shape) == 3:
            return ref.at[which] if rows is None else ref.at[which, rows]
        lanes = pl.ds(pl.multiple_of(which * half, half), half)
        return ref.at[:, lanes] if rows is None else ref.at[rows, lanes]

    sends = []

    def begin(copy):
        copy.start()
        sends.append(copy)
        return copy

    def to_sib(j, block, send, recv):
        return begin(push(wbuf.at[j, block, mine], wbuf.at[j, block, mine], send, recv, "cand", sib))

    def send_a(j):
        return begin(push(part(weights[j], 1 - x, mine), wbuf.at[j, u, mine],
                          a_s.at[j], a_r.at[j], "user", mate))

    def send_b(j):
        return [
            begin(push(part(weights[j], x, mine), wbuf.at[j, u, mine],
                       b_s.at[j, dq - 1], b_r.at[j, dq - 1], "user", above(dq)))
            for dq in others
        ]

    def send_c(j):
        return [
            begin(push(wbuf.at[j, mate, mine], wbuf.at[j, mate, mine],
                       c_s.at[j, dq - 1], c_r.at[j, dq - 1], "user", above(dq)))
            for dq in others
        ]

    rows_half = tokens // 2
    piece = rows_half // chunks
    first = lax.rem(g, 2)

    def piece_rows(which, i):
        return pl.ds(pl.multiple_of(which * rows_half + i * piece, piece), piece)

    def send_n(i):
        return begin(push(states_ref.at[piece_rows(first, i)], part_raw.at[piece_rows(first, i)],
                          n_s.at[i], n_r.at[i], "user", mate))

    def send_z(i):
        return begin(push(part_raw.at[piece_rows(first, i)], part_raw.at[piece_rows(first, i)],
                          z_s.at[i], z_r.at[i], "gen", gen_mate))

    per = n_user // n_gen
    owner = u // per
    far = jnp.where(g > owner, g - owner, owner - g)
    p_rows = proj.shape[0] // n_cand
    proj_mine = proj.at[pl.ds(pl.multiple_of(c * p_rows, p_rows), p_rows)]
    p_at = pl.ds(pl.multiple_of(lax.rem(u, per) * (n_cand * p_rows) + c * p_rows, p_rows), p_rows)

    def proj_up():
        return push(proj_mine, proj_mine, p_s.at[0], p_r.at[0], "gen", lax.rem(g + 1, n_gen))

    def proj_down():
        return push(proj_mine, proj_mine, p_s.at[1], p_r.at[0], "gen", lax.rem(g + n_gen - 1, n_gen))

    goes_up = jnp.logical_and(g >= owner, g < n_gen - 1)
    goes_down = jnp.logical_and(g <= owner, g > 0)

    def proj_pass():
        @pl.when(goes_up)
        def _():
            proj_up().start()

        @pl.when(goes_down)
        def _():
            proj_down().start()

    def proj_step(k):
        @pl.when(far == k)
        def _():
            proj_up().wait_recv()
            proj_pass()

    a0, b0 = send_a(0), send_b(0)
    locals_ = []
    for j in range(2):
        copy = pltpu.make_async_copy(part(weights[j], x, None), wbuf.at[j, u], loc.at[j])
        copy.start()
        locals_.append(copy)

    down_copy = pltpu.make_async_copy(down_ref, down, loc.at[3])
    down_copy.start()

    @pl.when(far == 0)
    def _():
        copy = pltpu.make_async_copy(proj_ref.at[p_at], proj_mine, loc.at[2])
        copy.start()
        copy.wait()
        proj_pass()

    step = 64

    def norm_own(i, _):
        rows = pl.ds(pl.multiple_of(i * step, step), step)
        norm[rows] = normalise(states_ref[rows], gain_ref[...])
        return 0

    def norm_part(i):
        n_at = tokens + 2 * i * piece
        norm[n_at:n_at + piece] = normalise(part_raw[piece_rows(first, i)], gain_ref[...])
        z_copies[i].wait_recv()
        norm[n_at + piece:n_at + 2 * piece] = normalise(
            part_raw[piece_rows(1 - first, i)], gain_ref[...]
        )

    def dots(j, block, low, high, start=False):
        lanes = pl.ds(pl.multiple_of(block * depth, depth), depth)
        term = jnp.dot(norm[low:high, lanes], wbuf[j, block], preferred_element_type=F32)
        acc[j, low:high] = term if start else acc[j, low:high] + term

    lax.fori_loop(0, tokens // step, norm_own, 0)
    for copy in locals_:
        copy.wait()
    for j in range(2):
        dots(j, u, 0, tokens, True)

    groups = tokens // STEPS
    slab = proj_ref.shape[0]
    own_cols = states_ref[:, pl.ds(pl.multiple_of(g * slab, slab), slab)]
    pooled_in = jnp.dot(pool_matrix(groups), own_cols, preferred_element_type=F32).astype(BF16)
    e_own[...] = jnp.dot(pooled_in, proj_ref[...], preferred_element_type=F32)
    encoded[...] = unit_rows(jnp.dot(rows_ref[...], encw_ref[...], preferred_element_type=F32))

    early = tokens + (chunks // 2) * 2 * piece
    sib_b, n_copies, z_copies = [], [], []

    def pass_n(i):
        n_copies[i].wait_recv()
        z_copies.append(send_z(i))

    a0.wait_recv()
    n_copies += [send_n(0), send_n(1)]
    c0 = send_c(0)
    b1 = send_b(1)
    sib_a0 = to_sib(0, mate, sa_s.at[0], sa_r.at[0])
    for dq in others:
        b0[dq - 1].wait_recv()
        sib_b.append(to_sib(0, below(dq) + x, sb_s.at[0, dq - 1], sb_r.at[0, dq - 1]))
    pass_n(0)
    a1 = send_a(1)
    pass_n(1)
    n_copies.append(send_n(2))
    proj_step(1)
    sib_a0.wait_recv()
    dots(0, mate, 0, tokens)
    for dq in others:
        b1[dq - 1].wait_recv()
        sib_b.append(to_sib(1, below(dq) + x, sb_s.at[1, dq - 1], sb_r.at[1, dq - 1]))
    a1.wait_recv()
    n_copies.append(send_n(3))
    c1 = send_c(1)
    sib_a1 = to_sib(1, mate, sa_s.at[1], sa_r.at[1])
    proj_step(2)
    for copy in sib_b:
        copy.wait_recv()
    for dq in others:
        for j in range(2):
            dots(j, below(dq) + x, 0, tokens)
    pass_n(2)
    for i in range(chunks // 2):
        norm_part(i)
    for j in range(2):
        dots(j, u, tokens, early, True)
    sib_c = []
    for dq in others:
        c0[dq - 1].wait_recv()
        sib_c.append(to_sib(0, below(dq) + 1 - x, sc_s.at[0, dq - 1], sc_r.at[0, dq - 1]))
    dots(0, mate, tokens, early)
    sib_a1.wait_recv()
    dots(1, mate, 0, early)
    pass_n(3)
    for k in range(3, n_gen):
        proj_step(k)
    begin(push(proj_mine, proj_mine, pj_s.at[0], pj_r.at[0], "cand", sib))
    for dq in others:
        for j in range(2):
            dots(j, below(dq) + x, tokens, early)
    for copy in sib_c:
        copy.wait_recv()
    for dq in others:
        dots(0, below(dq) + 1 - x, 0, early)
    norm_part(2)
    sib_c = []
    for dq in others:
        c1[dq - 1].wait_recv()
        sib_c.append(to_sib(1, below(dq) + 1 - x, sc_s.at[1, dq - 1], sc_r.at[1, dq - 1]))
    for copy in sib_c:
        copy.wait_recv()
    for dq in others:
        dots(1, below(dq) + 1 - x, 0, early)

    out_rows = 2 * piece // STEPS
    small = out_rows // 2
    pool = pool_matrix(out_rows)

    def pooled(gate, up):
        hidden = (jax.nn.silu(gate) * up).astype(BF16)
        return jnp.dot(pool, hidden, preferred_element_type=F32).astype(BF16)

    def own_out(i, _):
        rows = pl.ds(pl.multiple_of(i * 2 * piece, 2 * piece), 2 * piece)
        at = pl.multiple_of(x * groups + i * out_rows, out_rows)
        ph_in[u, pl.ds(at, out_rows)] = pooled(acc[0, rows], acc[1, rows])
        return 0

    def part_out(i, out):
        for k, which in enumerate((first, 1 - first)):
            at = pl.multiple_of(
                (1 - x) * groups + which * (rows_half // STEPS) + i * small, small
            )
            ph_in[u, pl.ds(at, small)] = out[k * small:(k + 1) * small]

    def send_ph(part_at, start, size):
        rows = pl.ds(pl.multiple_of(start, size), size)
        for dq, dx in [(dq, dx) for dq in range(cols) for dx in range(2)][1:]:
            k = dq * 2 + dx - 1
            peer = lax.rem(q + dq, cols) * 2 + lax.rem(x + dx, 2)
            begin(push(ph_in.at[u, rows], ph_in.at[u, rows], ph_s.at[part_at, k],
                       ph_r.at[part_at, k], "user", peer))

    quarter = groups // 4
    lax.fori_loop(0, tokens // (2 * piece), own_out, 0)
    send_ph(0, x * groups, groups)
    for i in range(chunks // 2):
        rows = slice(tokens + 2 * i * piece, tokens + 2 * (i + 1) * piece)
        part_out(i, pooled(acc[0, rows], acc[1, rows]))
    for k in range(2):
        send_ph(1 + k, (1 - x) * groups + 2 * k * quarter, quarter)
    norm_part(3)
    both = []
    for j in range(2):
        total = None
        for block in range(n_user):
            term = jnp.dot(norm[early:, block * depth:(block + 1) * depth], wbuf[j, block],
                           preferred_element_type=F32)
            total = term if total is None else total + term
        both.append(total)
    for i in range(chunks // 2, chunks):
        rows = slice(2 * i * piece + tokens - early, 2 * (i + 1) * piece + tokens - early)
        part_out(i, pooled(both[0][rows], both[1][rows]))

    for k in range(2):
        send_ph(3 + k, (1 - x) * groups + (2 * k + 1) * quarter, quarter)
    down_copy.wait()

    def finish():
        for copy in sends:
            copy.wait_send()

        @pl.when(goes_up)
        def _():
            proj_up().wait_send()

        @pl.when(goes_down)
        def _():
            proj_down().wait_send()

    return finish


def tail_part(
    n_gen, n_user, n_cand, ratio,
    ids_col, ids_row, out_ref,
    ph_in, proj, e_own, down_ref, enc_ref, rs_out, rs_in, zr_out, zr_in, cz, call_in, kern,
    tot_out, tot_in, vote_mine, vote_u_in, vote_g_mine, vote_g_in,
    pj_s, pj_r, ph_s, ph_r, rs_s, rs_r, zr_s, zr_r, cz_s, cz_r, ca_s, ca_r,
    tot_s, tot_r, vu_s, vu_r, vg_s, vg_r,
):
    u = lax.axis_index("user")
    g = lax.axis_index("gen")
    c = lax.axis_index("cand")
    sib = lax.rem(c + 1, n_cand)
    groups = e_own.shape[0]
    half = ph_in.shape[2]
    cols = n_user // 2
    q, x = u // 2, lax.rem(u, 2)

    def peer_u(k):
        return lax.rem(u + k, n_user)

    def peer_g(k):
        return lax.rem(g + k, n_gen)

    shifts = [(dq, dx) for dq in range(cols) for dx in range(2)][1:]
    quarter = groups // 4

    def ph_wait(dq, dx):
        k = dq * 2 + dx - 1
        for part_at in range(5):
            rows = pl.ds(0, groups if part_at == 0 else quarter)
            push(ph_in.at[u, rows], ph_in.at[u, rows], ph_s.at[part_at, k],
                 ph_r.at[part_at, k], "user", lax.rem(u + 1, n_user)).wait_recv()

    p_rows = proj.shape[0] // n_cand
    proj_half = proj.at[pl.ds(0, p_rows)]
    push(proj_half, proj_half, pj_s.at[0], pj_r.at[0], "cand", sib).wait_recv()

    def rs_copy(dq, dx):
        k = dq * 2 + dx - 1
        peer = lax.rem(q + cols - dq, cols) * 2 + lax.rem(x + dx, 2)
        return push(rs_out.at[k], rs_in.at[k], rs_s.at[k], rs_r.at[k], "user", peer)

    def embed(dq):
        there = lax.rem(q + cols - dq, cols) * 2
        mixed = jnp.dot(ph_in[there], down_ref[:half], preferred_element_type=F32)
        mixed += jnp.dot(ph_in[there + 1], down_ref[half:], preferred_element_type=F32)
        full = jnp.dot(mixed.astype(BF16), proj[...], preferred_element_type=F32)
        near = jnp.where(x == 0, full[:groups], full[groups:])
        far = jnp.where(x == 0, full[groups:], full[:groups])
        return near, far

    ph_wait(0, 1)
    near, far = embed(0)
    rs_out[0] = far.astype(BF16)
    rs_copy(0, 1).start()
    e_own[...] += near

    def step(dq, _):
        ph_wait(dq, 0)
        ph_wait(dq, 1)
        near, far = embed(dq)
        rs_out[dq * 2 - 1] = near.astype(BF16)
        rs_copy(dq, 0).start()
        rs_out[dq * 2] = far.astype(BF16)
        rs_copy(dq, 1).start()
        return 0

    lax.fori_loop(1, cols, step, 0)
    total = e_own[...]
    for dq, dx in shifts:
        rs_copy(dq, dx).wait_recv()
        total = total + rs_in[dq * 2 + dx - 1].astype(F32)

    share = groups // n_gen
    zr_out[...] = total.reshape(n_gen, share, total.shape[1])
    own_sum = zr_out[g]
    zr_copy = []
    for k in range(1, n_gen):
        cz[k] = zr_out[peer_g(k)].astype(BF16)
        copy = push(cz.at[k], zr_in.at[k - 1], zr_s.at[k - 1], zr_r.at[k - 1], "gen", peer_g(k))
        copy.start()
        zr_copy.append(copy)
    for k in range(1, n_gen):
        zr_copy[k - 1].wait_recv()
        own_sum = own_sum + zr_in[k - 1].astype(F32)
    own_sum = own_sum * (1.0 / STEPS)
    cz[0] = unit_rows(own_sum)

    cg_copy = []
    for k in range(1, n_gen):
        copy = push(cz.at[0], call_in.at[0, pl.ds(pl.multiple_of(g * share, share), share)],
                    cz_s.at[k - 1], cz_r.at[k - 1], "gen", peer_g(k))
        copy.start()
        cg_copy.append(copy)
    call_in[0, pl.ds(pl.multiple_of(g * share, share), share)] = cz[0]
    for copy in cg_copy:
        copy.wait_recv()
    ca_copy = []
    for k in range(1, n_user):
        copy = push(call_in.at[0], call_in.at[k], ca_s.at[k - 1], ca_r.at[k - 1], "user", peer_u(k))
        copy.start()
        ca_copy.append(copy)

    def score(k):
        scores = lax.dot_general(
            enc_ref[...], call_in[k], (((1,), (1,)), ((), ())), preferred_element_type=F32
        )
        value = jnp.exp(scores * 60.0)
        kern[k] = value
        return jnp.sum(value, axis=1, keepdims=True)

    totals = score(0)
    for k in range(1, n_user):
        ca_copy[k - 1].wait_recv()
        totals = totals + score(k)
    tot_out[...] = jnp.broadcast_to(totals, tot_out.shape)
    tot_copy = push(tot_out, tot_in, tot_s.at[0], tot_r.at[0], "cand", sib)
    tot_copy.start()
    tot_copy.wait_recv()
    totals = totals + tot_in[:, :1]
    counts = jnp.sum((ids_col[...] == ids_row[...]).astype(F32), axis=1, keepdims=True)
    weight = jnp.minimum(1.0, CAP / counts) / totals * ratio
    for k in range(n_user):
        part = jnp.sum(kern[k] * weight, axis=0, keepdims=True)
        vote_mine[lax.rem(u + n_user - k, n_user)] = jnp.broadcast_to(part, vote_mine.shape[1:])

    vu_copy = []
    for k in range(1, n_user):
        copy = push(vote_mine, vote_u_in.at[k - 1], vu_s.at[k - 1], vu_r.at[k - 1], "user", peer_u(k))
        copy.start()
        vu_copy.append(copy)
    votes = vote_mine[...]
    for k in range(1, n_user):
        vu_copy[k - 1].wait_recv()
        votes = votes + vote_u_in[k - 1]
    vote_g_mine[...] = votes
    vg_copy = []
    for k in range(1, n_gen):
        copy = push(vote_g_mine, vote_g_in.at[k - 1], vg_s.at[k - 1], vg_r.at[k - 1], "gen", peer_g(k))
        copy.start()
        vg_copy.append(copy)
    for k in range(1, n_gen):
        vg_copy[k - 1].wait_recv()
        votes = votes + vote_g_in[k - 1]
    out_ref[...] = votes[:, :1, :]

    for copy in zr_copy + cg_copy + ca_copy + [tot_copy] + vu_copy + vg_copy:
        copy.wait_send()
    for shift in shifts:
        rs_copy(*shift).wait_send()


def split_columns(weight):
    half = weight.shape[1] // 2
    if half % 128 == 0:
        return weight
    return weight.reshape(weight.shape[0], 2, half).transpose(1, 0, 2)


def fused_kernel(n_gen, n_user, n_cand, chunks, ratio, *refs):
    ins, refs = refs[:10], refs[10:]
    out_ref, refs = refs[0], refs[1:]
    shared, refs = refs[:5], refs[5:]
    head_own, refs = refs[:23], refs[23:]
    (pj_s, pj_r, ph_s, ph_r), tail_own = refs[:4], refs[4:]
    sizes = (n_gen, n_user, n_cand)
    finish = head_part(*sizes, chunks, *ins[:8], *shared, *head_own, pj_s, pj_r, ph_s, ph_r)
    tail_part(
        *sizes, ratio, *ins[8:], out_ref, *shared, *tail_own[:TAIL_BUFFERS],
        pj_s, pj_r, ph_s, ph_r, *tail_own[TAIL_BUFFERS:],
    )
    finish()


def fused(states, norm_gain, gate_weight, up_weight, proj_weight, down_weight, private_rows,
          enc_weight, user_ids, ratio):
    n_gen, n_user, n_cand = (lax.axis_size(a) for a in ("gen", "user", "cand"))
    tokens, width = states.shape
    groups = tokens // STEPS
    depth, half = gate_weight.shape[0], gate_weight.shape[1] // 2
    emb = proj_weight.shape[1]
    rows = private_rows.shape[0]
    share = groups // n_gen
    chunks = 4
    cols = n_user // 2
    nu, ng = n_user - 1, n_gen - 1
    vmem = pltpu.VMEM
    dma = pltpu.SemaphoreType.DMA
    many = dma((2, cols - 1))
    anywhere = pl.BlockSpec(memory_space=pl.ANY)
    inside = pl.BlockSpec(memory_space=vmem)
    return pl.pallas_call(
        functools.partial(fused_kernel, n_gen, n_user, n_cand, chunks, ratio),
        out_shape=jax.ShapeDtypeStruct((n_user, 1, groups), F32),
        in_specs=[inside, inside, anywhere, anywhere, inside, anywhere] + [inside] * 4,
        out_specs=inside,
        scratch_shapes=[
            vmem((n_user, 2 * groups, half), BF16),
            vmem((proj_weight.shape[0] * n_gen // n_user, emb), BF16),
            vmem((groups, emb), F32),
            vmem(down_weight.shape, BF16),
            vmem((rows, emb), BF16),
            vmem((2, n_user, depth, half), BF16),
            vmem((2 * tokens, width), BF16),
            vmem((tokens, width), BF16),
            vmem((2, tokens + tokens // 2, half), F32),
            dma((4,)),
            dma((2,)), dma((2,)), many, many, many, many,
            dma((2,)), dma((2,)), many, many, many, many,
            dma((chunks,)), dma((chunks,)), dma((chunks,)), dma((chunks,)),
            dma((2,)), dma((1,)),
            dma((1,)), dma((1,)),
            dma((5, nu)), dma((5, nu)),
            vmem((nu, groups, emb), BF16),
            vmem((nu, groups, emb), BF16),
            vmem((n_gen, share, emb), F32),
            vmem((ng, share, emb), BF16),
            vmem((n_gen, share, emb), BF16),
            vmem((n_user, groups, emb), BF16),
            vmem((n_user, rows, groups), F32),
            vmem((rows, 128), F32),
            vmem((rows, 128), F32),
            vmem((n_user, 8, groups), F32),
            vmem((nu, n_user, 8, groups), F32),
            vmem((n_user, 8, groups), F32),
            vmem((ng, n_user, 8, groups), F32),
            dma((nu,)), dma((nu,)),
            dma((ng,)), dma((ng,)),
            dma((ng,)), dma((ng,)),
            dma((nu,)), dma((nu,)),
            dma((1,)), dma((1,)),
            dma((nu,)), dma((nu,)),
            dma((ng,)), dma((ng,)),
        ],
        compiler_params=pltpu.CompilerParams(
            collective_id=0, has_side_effects=True, vmem_limit_bytes=62 * 1024 * 1024
        ),
    )(states, norm_gain.reshape(1, width), split_columns(gate_weight), split_columns(up_weight),
      proj_weight, down_weight, private_rows, enc_weight,
      user_ids.reshape(rows, 1), user_ids.reshape(1, rows))


def shards(
    states,
    norm_gain,
    gate_weight,
    up_weight,
    down_weight,
    proj_weight,
    private_rows,
    enc_weight,
    user_ids,
):
    groups = states.shape[0] // STEPS
    row_total = private_rows.shape[0] * lax.axis_size("gen") * lax.axis_size("user")
    cand_total = groups * lax.axis_size("user") * lax.axis_size("cand")
    return fused(states, norm_gain, gate_weight, up_weight, proj_weight, down_weight,
                 private_rows, enc_weight, user_ids, cand_total / row_total)


def solution(mesh):
    return jax.shard_map(
        shards,
        mesh=mesh,
        in_specs=(
            P(("user", "cand"), None),
            P(),
            P("user", "gen"),
            P("user", "gen"),
            P("gen", "user"),
            P("gen", None),
            P(("gen", "user"), None),
            P(),
            P(("gen", "user")),
        ),
        out_specs=P(None, "cand", None),
        check_vma=False,
    )
```

```python
import functools

import jax
import jax.numpy as jnp
from jax import lax
from jax.experimental import pallas as pl
from jax.experimental.pallas import tpu as pltpu
from jax.sharding import PartitionSpec as P

STEPS = 4
CAP = 8
TAIL_BUFFERS = 13
F32 = jnp.float32
BF16 = jnp.bfloat16
MESH = pl.DeviceIdType.MESH


def unit_rows(matrix):
    return (matrix * lax.rsqrt(jnp.sum(matrix * matrix, axis=1, keepdims=True) + 1e-06)).astype(BF16)


def pool_matrix(groups):
    rows = lax.broadcasted_iota(jnp.int32, (groups, groups * STEPS), 0)
    cols = lax.broadcasted_iota(jnp.int32, (groups, groups * STEPS), 1)
    return (cols // STEPS == rows).astype(BF16)


def greet(sizes):
    barrier = pltpu.get_barrier_semaphore()
    count = 0
    for axis, size in sizes:
        me = lax.axis_index(axis)
        for k in range(1, size):
            pl.semaphore_signal(
                barrier, inc=1, device_id={axis: lax.rem(me + k, size)}, device_id_type=MESH
            )
            count += 1
    pl.semaphore_wait(barrier, count)


def push(src, dst, send, recv, axis, peer):
    return pltpu.make_async_remote_copy(
        src_ref=src, dst_ref=dst, send_sem=send, recv_sem=recv,
        device_id={axis: peer}, device_id_type=MESH,
    )


def normalise(block, gain):
    values = block.astype(F32)
    scale = lax.rsqrt(jnp.mean(values * values, axis=1, keepdims=True) + 1e-05)
    return (values * scale * gain).astype(BF16)


def head_part(
    n_gen, n_user, n_cand, chunks,
    states_ref, gain_ref, gate_ref, up_ref, proj_ref, down_ref, rows_ref, encw_ref,
    ids_col, ids_row,
    ph_in, proj, e_own, down, enc_all, cap_all,
    wbuf, norm, part_raw, acc,
    loc, a_s, a_r, b_s, b_r, c_s, c_r, sa_s, sa_r, sb_s, sb_r, sc_s, sc_r, n_s, n_r, z_s, z_r,
    p_s, p_r, en_s, en_r, es_s, es_r, cp_s, cp_r, pj_s, pj_r, ph_s, ph_r,
):
    u = lax.axis_index("user")
    g = lax.axis_index("gen")
    c = lax.axis_index("cand")
    cols = n_user // 2
    q, x = u // 2, lax.rem(u, 2)
    mate = q * 2 + 1 - x
    gen_mate = (g // 2) * 2 + 1 - lax.rem(g, 2)
    sib = lax.rem(c + 1, n_cand)
    tokens, width = states_ref.shape
    depth, half = wbuf.shape[2], wbuf.shape[3]
    share = depth // n_cand
    mine = pl.ds(pl.multiple_of(c * share, share), share)
    weights = (gate_ref, up_ref)
    others = range(1, cols)

    def above(dq):
        return lax.rem(q + dq, cols) * 2 + x

    def below(dq):
        return lax.rem(q + cols - dq, cols) * 2

    greet((("user", n_user), ("gen", n_gen), ("cand", n_cand)))

    def part(ref, which, rows):
        if len(ref.shape) == 3:
            return ref.at[which] if rows is None else ref.at[which, rows]
        lanes = pl.ds(pl.multiple_of(which * half, half), half)
        return ref.at[:, lanes] if rows is None else ref.at[rows, lanes]

    sends = []

    def begin(copy):
        copy.start()
        sends.append(copy)
        return copy

    def to_sib(j, block, send, recv):
        return begin(push(wbuf.at[j, block, mine], wbuf.at[j, block, mine], send, recv, "cand", sib))

    def send_a(j):
        return begin(push(part(weights[j], 1 - x, mine), wbuf.at[j, u, mine],
                          a_s.at[j], a_r.at[j], "user", mate))

    def send_b(j):
        return [
            begin(push(part(weights[j], x, mine), wbuf.at[j, u, mine],
                       b_s.at[j, dq - 1], b_r.at[j, dq - 1], "user", above(dq)))
            for dq in others
        ]

    def send_c(j):
        return [
            begin(push(wbuf.at[j, mate, mine], wbuf.at[j, mate, mine],
                       c_s.at[j, dq - 1], c_r.at[j, dq - 1], "user", above(dq)))
            for dq in others
        ]

    rows_half = tokens // 2
    piece = rows_half // chunks
    first = lax.rem(g, 2)

    def piece_rows(which, i):
        return pl.ds(pl.multiple_of(which * rows_half + i * piece, piece), piece)

    def send_n(i):
        return begin(push(states_ref.at[piece_rows(first, i)], part_raw.at[piece_rows(first, i)],
                          n_s.at[i], n_r.at[i], "user", mate))

    def send_z(i):
        return begin(push(part_raw.at[piece_rows(first, i)], part_raw.at[piece_rows(first, i)],
                          z_s.at[i], z_r.at[i], "gen", gen_mate))

    per = n_user // n_gen
    owner = u // per
    far = jnp.where(g > owner, g - owner, owner - g)
    p_rows = proj.shape[0] // n_cand
    proj_mine = proj.at[pl.ds(pl.multiple_of(c * p_rows, p_rows), p_rows)]
    p_at = pl.ds(pl.multiple_of(lax.rem(u, per) * (n_cand * p_rows) + c * p_rows, p_rows), p_rows)

    def proj_up():
        return push(proj_mine, proj_mine, p_s.at[0], p_r.at[0], "gen", lax.rem(g + 1, n_gen))

    def proj_down():
        return push(proj_mine, proj_mine, p_s.at[1], p_r.at[0], "gen", lax.rem(g + n_gen - 1, n_gen))

    goes_up = jnp.logical_and(g >= owner, g < n_gen - 1)
    goes_down = jnp.logical_and(g <= owner, g > 0)

    def proj_pass():
        @pl.when(goes_up)
        def _():
            proj_up().start()

        @pl.when(goes_down)
        def _():
            proj_down().start()

    def proj_step(k):
        @pl.when(far == k)
        def _():
            proj_up().wait_recv()
            proj_pass()

    a0, b0 = send_a(0), send_b(0)
    locals_ = []
    for j in range(2):
        copy = pltpu.make_async_copy(part(weights[j], x, None), wbuf.at[j, u], loc.at[j])
        copy.start()
        locals_.append(copy)

    down_copy = pltpu.make_async_copy(down_ref, down, loc.at[3])
    down_copy.start()

    @pl.when(far == 0)
    def _():
        copy = pltpu.make_async_copy(proj_ref.at[p_at], proj_mine, loc.at[2])
        copy.start()
        copy.wait()
        proj_pass()

    step = 64

    def norm_own(i, _):
        rows = pl.ds(pl.multiple_of(i * step, step), step)
        norm[rows] = normalise(states_ref[rows], gain_ref[...])
        return 0

    def norm_part(i):
        n_at = tokens + 2 * i * piece
        norm[n_at:n_at + piece] = normalise(part_raw[piece_rows(first, i)], gain_ref[...])
        z_copies[i].wait_recv()
        norm[n_at + piece:n_at + 2 * piece] = normalise(
            part_raw[piece_rows(1 - first, i)], gain_ref[...]
        )

    def dots(j, block, low, high, start=False):
        lanes = pl.ds(pl.multiple_of(block * depth, depth), depth)
        term = jnp.dot(norm[low:high, lanes], wbuf[j, block], preferred_element_type=F32)
        acc[j, low:high] = term if start else acc[j, low:high] + term

    lax.fori_loop(0, tokens // step, norm_own, 0)
    for copy in locals_:
        copy.wait()
    for j in range(2):
        dots(j, u, 0, tokens, True)

    groups = tokens // STEPS
    slab = proj_ref.shape[0]
    own_cols = states_ref[:, pl.ds(pl.multiple_of(g * slab, slab), slab)]
    pooled_in = jnp.dot(pool_matrix(groups), own_cols, preferred_element_type=F32).astype(BF16)
    e_own[...] = jnp.dot(pooled_in, proj_ref[...], preferred_element_type=F32)
    enc_all[g] = unit_rows(jnp.dot(rows_ref[...], encw_ref[...], preferred_element_type=F32))
    counts = jnp.sum((ids_col[...] == ids_row[...]).astype(F32), axis=0, keepdims=True)
    cap_all[g] = jnp.broadcast_to(jnp.minimum(1.0, CAP / counts), cap_all.shape[1:])
    e_rows = enc_all.shape[1] // n_cand
    e_mine = pl.ds(pl.multiple_of(c * e_rows, e_rows), e_rows)
    enc_copies = []
    for k in range(1, n_gen):
        peer = lax.rem(g + k, n_gen)
        enc_copies.append(begin(push(enc_all.at[g, e_mine], enc_all.at[g, e_mine],
                                     en_s.at[k - 1], en_r.at[k - 1], "gen", peer)))
        begin(push(cap_all.at[g], cap_all.at[g], cp_s.at[k - 1], cp_r.at[k - 1], "gen", peer))

    early = tokens + (chunks // 2) * 2 * piece
    sib_b, n_copies, z_copies = [], [], []

    def pass_n(i):
        n_copies[i].wait_recv()
        z_copies.append(send_z(i))

    a0.wait_recv()
    n_copies += [send_n(0), send_n(1)]
    c0 = send_c(0)
    b1 = send_b(1)
    sib_a0 = to_sib(0, mate, sa_s.at[0], sa_r.at[0])
    for dq in others:
        b0[dq - 1].wait_recv()
        sib_b.append(to_sib(0, below(dq) + x, sb_s.at[0, dq - 1], sb_r.at[0, dq - 1]))
    pass_n(0)
    a1 = send_a(1)
    pass_n(1)
    n_copies.append(send_n(2))
    proj_step(1)
    sib_a0.wait_recv()
    dots(0, mate, 0, tokens)
    for dq in others:
        b1[dq - 1].wait_recv()
        sib_b.append(to_sib(1, below(dq) + x, sb_s.at[1, dq - 1], sb_r.at[1, dq - 1]))
    a1.wait_recv()
    n_copies.append(send_n(3))
    c1 = send_c(1)
    sib_a1 = to_sib(1, mate, sa_s.at[1], sa_r.at[1])
    proj_step(2)
    for copy in sib_b:
        copy.wait_recv()
    for dq in others:
        for j in range(2):
            dots(j, below(dq) + x, 0, tokens)
    pass_n(2)
    for i in range(chunks // 2):
        norm_part(i)
    for j in range(2):
        dots(j, u, tokens, early, True)
    sib_c = []
    for dq in others:
        c0[dq - 1].wait_recv()
        sib_c.append(to_sib(0, below(dq) + 1 - x, sc_s.at[0, dq - 1], sc_r.at[0, dq - 1]))
    dots(0, mate, tokens, early)
    sib_a1.wait_recv()
    dots(1, mate, 0, early)
    pass_n(3)
    for k in range(1, n_gen):
        enc_copies[k - 1].wait_recv()
        there = lax.rem(g + n_gen - k, n_gen)
        begin(push(enc_all.at[there, e_mine], enc_all.at[there, e_mine],
                   es_s.at[k - 1], es_r.at[k - 1], "cand", sib))
    for k in range(3, n_gen):
        proj_step(k)
    begin(push(proj_mine, proj_mine, pj_s.at[0], pj_r.at[0], "cand", sib))
    for dq in others:
        for j in range(2):
            dots(j, below(dq) + x, tokens, early)
    for copy in sib_c:
        copy.wait_recv()
    for dq in others:
        dots(0, below(dq) + 1 - x, 0, early)
    norm_part(2)
    sib_c = []
    for dq in others:
        c1[dq - 1].wait_recv()
        sib_c.append(to_sib(1, below(dq) + 1 - x, sc_s.at[1, dq - 1], sc_r.at[1, dq - 1]))
    for copy in sib_c:
        copy.wait_recv()
    for dq in others:
        dots(1, below(dq) + 1 - x, 0, early)

    out_rows = 2 * piece // STEPS
    small = out_rows // 2
    pool = pool_matrix(out_rows)

    def pooled(gate, up):
        hidden = (jax.nn.silu(gate) * up).astype(BF16)
        return jnp.dot(pool, hidden, preferred_element_type=F32).astype(BF16)

    def own_out(i, _):
        rows = pl.ds(pl.multiple_of(i * 2 * piece, 2 * piece), 2 * piece)
        at = pl.multiple_of(x * groups + i * out_rows, out_rows)
        ph_in[u, pl.ds(at, out_rows)] = pooled(acc[0, rows], acc[1, rows])
        return 0

    def part_out(i, out):
        for k, which in enumerate((first, 1 - first)):
            at = pl.multiple_of(
                (1 - x) * groups + which * (rows_half // STEPS) + i * small, small
            )
            ph_in[u, pl.ds(at, small)] = out[k * small:(k + 1) * small]

    def send_ph(part_at, start, size):
        rows = pl.ds(pl.multiple_of(start, size), size)
        for dq, dx in [(dq, dx) for dq in range(cols) for dx in range(2)][1:]:
            k = dq * 2 + dx - 1
            peer = lax.rem(q + dq, cols) * 2 + lax.rem(x + dx, 2)
            begin(push(ph_in.at[u, rows], ph_in.at[u, rows], ph_s.at[part_at, k],
                       ph_r.at[part_at, k], "user", peer))

    quarter = groups // 4
    lax.fori_loop(0, tokens // (2 * piece), own_out, 0)
    send_ph(0, x * groups, groups)
    for i in range(chunks // 2):
        rows = slice(tokens + 2 * i * piece, tokens + 2 * (i + 1) * piece)
        part_out(i, pooled(acc[0, rows], acc[1, rows]))
    for k in range(2):
        send_ph(1 + k, (1 - x) * groups + 2 * k * quarter, quarter)
    norm_part(3)
    both = []
    for j in range(2):
        total = None
        for block in range(n_user):
            term = jnp.dot(norm[early:, block * depth:(block + 1) * depth], wbuf[j, block],
                           preferred_element_type=F32)
            total = term if total is None else total + term
        both.append(total)
    for i in range(chunks // 2, chunks):
        rows = slice(2 * i * piece + tokens - early, 2 * (i + 1) * piece + tokens - early)
        part_out(i, pooled(both[0][rows], both[1][rows]))

    for k in range(2):
        send_ph(3 + k, (1 - x) * groups + (2 * k + 1) * quarter, quarter)
    down_copy.wait()

    def finish():
        for copy in sends:
            copy.wait_send()

        @pl.when(goes_up)
        def _():
            proj_up().wait_send()

        @pl.when(goes_down)
        def _():
            proj_down().wait_send()

    return finish


def tail_part(
    n_gen, n_user, n_cand, ratio,
    out_ref,
    ph_in, proj, e_own, down_ref, enc_all, cap_all, rs_out, rs_in, zr_out, zr_in, cz, call_in, kern,
    tot_out, tot_in, tot_sib, vote_mine, vote_u_in, vote_g_all,
    es_r, cp_r, pj_s, pj_r, ph_s, ph_r, rs_s, rs_r, zr_s, zr_r, ca_s, ca_r,
    tg_s, tg_r, tot_s, tot_r, vu_s, vu_r, vg_s, vg_r,
):
    u = lax.axis_index("user")
    g = lax.axis_index("gen")
    c = lax.axis_index("cand")
    sib = lax.rem(c + 1, n_cand)
    groups = e_own.shape[0]
    half = ph_in.shape[2]
    cols = n_user // 2
    q, x = u // 2, lax.rem(u, 2)

    def peer_u(k):
        return lax.rem(u + k, n_user)

    def peer_g(k):
        return lax.rem(g + k, n_gen)

    shifts = [(dq, dx) for dq in range(cols) for dx in range(2)][1:]
    quarter = groups // 4

    def ph_wait(dq, dx):
        k = dq * 2 + dx - 1
        for part_at in range(5):
            rows = pl.ds(0, groups if part_at == 0 else quarter)
            push(ph_in.at[u, rows], ph_in.at[u, rows], ph_s.at[part_at, k],
                 ph_r.at[part_at, k], "user", lax.rem(u + 1, n_user)).wait_recv()

    p_rows = proj.shape[0] // n_cand
    proj_half = proj.at[pl.ds(0, p_rows)]
    push(proj_half, proj_half, pj_s.at[0], pj_r.at[0], "cand", sib).wait_recv()

    def rs_copy(dq, dx):
        k = dq * 2 + dx - 1
        peer = lax.rem(q + cols - dq, cols) * 2 + lax.rem(x + dx, 2)
        return push(rs_out.at[k], rs_in.at[k], rs_s.at[k], rs_r.at[k], "user", peer)

    def embed(dq):
        there = lax.rem(q + cols - dq, cols) * 2
        mixed = jnp.dot(ph_in[there], down_ref[:half], preferred_element_type=F32)
        mixed += jnp.dot(ph_in[there + 1], down_ref[half:], preferred_element_type=F32)
        full = jnp.dot(mixed.astype(BF16), proj[...], preferred_element_type=F32)
        near = jnp.where(x == 0, full[:groups], full[groups:])
        far = jnp.where(x == 0, full[groups:], full[:groups])
        return near, far

    ph_wait(0, 1)
    near, far = embed(0)
    rs_out[0] = far.astype(BF16)
    rs_copy(0, 1).start()
    e_own[...] += near

    def step(dq, _):
        ph_wait(dq, 0)
        ph_wait(dq, 1)
        near, far = embed(dq)
        rs_out[dq * 2 - 1] = near.astype(BF16)
        rs_copy(dq, 0).start()
        rs_out[dq * 2] = far.astype(BF16)
        rs_copy(dq, 1).start()
        return 0

    lax.fori_loop(1, cols, step, 0)
    total = e_own[...]
    for dq, dx in shifts:
        rs_copy(dq, dx).wait_recv()
        total = total + rs_in[dq * 2 + dx - 1].astype(F32)

    share = groups // n_gen
    zr_out[...] = total.reshape(n_gen, share, total.shape[1])
    own_sum = zr_out[g]
    zr_copy = []
    for k in range(1, n_gen):
        cz[k] = zr_out[peer_g(k)].astype(BF16)
        copy = push(cz.at[k], zr_in.at[k - 1], zr_s.at[k - 1], zr_r.at[k - 1], "gen", peer_g(k))
        copy.start()
        zr_copy.append(copy)
    for k in range(1, n_gen):
        zr_copy[k - 1].wait_recv()
        own_sum = own_sum + zr_in[k - 1].astype(F32)
    own_sum = own_sum * (1.0 / STEPS)
    cz[0] = unit_rows(own_sum)

    call_in[u] = cz[0]
    ca_copy = []
    for k in range(1, n_user):
        copy = push(cz.at[0], call_in.at[u], ca_s.at[k - 1], ca_r.at[k - 1], "user", peer_u(k))
        copy.start()
        ca_copy.append(copy)
    for k in range(1, n_gen):
        half_rows = pl.ds(0, enc_all.shape[1] // n_cand)
        there = peer_g(k)
        push(enc_all.at[there, half_rows], enc_all.at[there, half_rows],
             es_r.at[k - 1], es_r.at[k - 1], "cand", sib).wait_recv()
        push(cap_all.at[there], cap_all.at[there],
             cp_r.at[k - 1], cp_r.at[k - 1], "gen", there).wait_recv()
    for copy in ca_copy:
        copy.wait_recv()
    every = call_in[...].reshape(n_user * share, call_in.shape[2])
    ones = jnp.ones((8, n_user * share), F32)
    for there in range(n_gen):
        scores = lax.dot_general(
            enc_all[there], every, (((1,), (1,)), ((), ())), preferred_element_type=F32
        )
        value = jnp.exp(scores * 60.0)
        kern[there] = value
        tot_out[there] = lax.dot_general(
            ones, value, (((1,), (1,)), ((), ())), preferred_element_type=F32,
            precision=lax.Precision.HIGHEST,
        )
    tot_copy = []
    for k in range(1, n_gen):
        copy = push(tot_out, tot_in.at[k - 1], tg_s.at[k - 1], tg_r.at[k - 1], "gen", peer_g(k))
        copy.start()
        tot_copy.append(copy)
    totals = tot_out[...]
    for k in range(1, n_gen):
        tot_copy[k - 1].wait_recv()
        totals = totals + tot_in[k - 1]
    tot_sib[0] = totals
    copy = push(tot_sib.at[0], tot_sib.at[1], tot_s.at[0], tot_r.at[0], "cand", sib)
    copy.start()
    tot_copy.append(copy)
    copy.wait_recv()
    weight = cap_all[...] / (totals + tot_sib[1]) * ratio
    votes = jnp.zeros(vote_mine.shape, F32)
    for there in range(n_gen):
        votes = votes + jnp.dot(
            weight[there], kern[there], preferred_element_type=F32,
            precision=lax.Precision.HIGHEST,
        )
    vote_mine[...] = votes
    vu_copy = []
    for k in range(1, n_user):
        copy = push(vote_mine, vote_u_in.at[k - 1], vu_s.at[k - 1], vu_r.at[k - 1], "user", peer_u(k))
        copy.start()
        vu_copy.append(copy)
    for k in range(1, n_user):
        vu_copy[k - 1].wait_recv()
        votes = votes + vote_u_in[k - 1]
    vote_g_all[g] = votes
    vg_copy = []
    for k in range(1, n_gen):
        copy = push(vote_g_all.at[g], vote_g_all.at[g], vg_s.at[k - 1], vg_r.at[k - 1], "gen", peer_g(k))
        copy.start()
        vg_copy.append(copy)
    for copy in vg_copy:
        copy.wait_recv()
    for k in range(n_user):
        for there in range(n_gen):
            out_ref[k, :, there * share:(there + 1) * share] = vote_g_all[
                there, :1, k * share:(k + 1) * share
            ]

    for copy in zr_copy + ca_copy + tot_copy + vu_copy + vg_copy:
        copy.wait_send()
    for shift in shifts:
        rs_copy(*shift).wait_send()


def split_columns(weight):
    half = weight.shape[1] // 2
    if half % 128 == 0:
        return weight
    return weight.reshape(weight.shape[0], 2, half).transpose(1, 0, 2)


def fused_kernel(n_gen, n_user, n_cand, chunks, ratio, *refs):
    ins, refs = refs[:10], refs[10:]
    out_ref, refs = refs[0], refs[1:]
    shared, refs = refs[:6], refs[6:]
    head_own, refs = refs[:29], refs[29:]
    (pj_s, pj_r, ph_s, ph_r), tail_own = refs[:4], refs[4:]
    sizes = (n_gen, n_user, n_cand)
    finish = head_part(*sizes, chunks, *ins, *shared, *head_own, pj_s, pj_r, ph_s, ph_r)
    tail_part(
        *sizes, ratio, out_ref, *shared, *tail_own[:TAIL_BUFFERS],
        head_own[26], head_own[28], pj_s, pj_r, ph_s, ph_r, *tail_own[TAIL_BUFFERS:],
    )
    finish()


def fused(states, norm_gain, gate_weight, up_weight, proj_weight, down_weight, private_rows,
          enc_weight, user_ids, ratio):
    n_gen, n_user, n_cand = (lax.axis_size(a) for a in ("gen", "user", "cand"))
    tokens, width = states.shape
    groups = tokens // STEPS
    depth, half = gate_weight.shape[0], gate_weight.shape[1] // 2
    emb = proj_weight.shape[1]
    rows = private_rows.shape[0]
    share = groups // n_gen
    chunks = 4
    cols = n_user // 2
    nu, ng = n_user - 1, n_gen - 1
    vmem = pltpu.VMEM
    dma = pltpu.SemaphoreType.DMA
    many = dma((2, cols - 1))
    anywhere = pl.BlockSpec(memory_space=pl.ANY)
    inside = pl.BlockSpec(memory_space=vmem)
    return pl.pallas_call(
        functools.partial(fused_kernel, n_gen, n_user, n_cand, chunks, ratio),
        out_shape=jax.ShapeDtypeStruct((n_user, 1, groups), F32),
        in_specs=[inside, inside, anywhere, anywhere, inside, anywhere] + [inside] * 4,
        out_specs=inside,
        scratch_shapes=[
            vmem((n_user, 2 * groups, half), BF16),
            vmem((proj_weight.shape[0] * n_gen // n_user, emb), BF16),
            vmem((groups, emb), F32),
            vmem(down_weight.shape, BF16),
            vmem((n_gen, rows, emb), BF16),
            vmem((n_gen, 8, rows), F32),
            vmem((2, n_user, depth, half), BF16),
            vmem((2 * tokens, width), BF16),
            vmem((tokens, width), BF16),
            vmem((2, tokens + tokens // 2, half), F32),
            dma((4,)),
            dma((2,)), dma((2,)), many, many, many, many,
            dma((2,)), dma((2,)), many, many, many, many,
            dma((chunks,)), dma((chunks,)), dma((chunks,)), dma((chunks,)),
            dma((2,)), dma((1,)),
            dma((ng,)), dma((ng,)), dma((ng,)), dma((ng,)), dma((ng,)), dma((ng,)),
            dma((1,)), dma((1,)),
            dma((5, nu)), dma((5, nu)),
            vmem((nu, groups, emb), BF16),
            vmem((nu, groups, emb), BF16),
            vmem((n_gen, share, emb), F32),
            vmem((ng, share, emb), BF16),
            vmem((n_gen, share, emb), BF16),
            vmem((n_user, share, emb), BF16),
            vmem((n_gen, rows, n_user * share), F32),
            vmem((n_gen, 8, rows), F32),
            vmem((ng, n_gen, 8, rows), F32),
            vmem((2, n_gen, 8, rows), F32),
            vmem((8, n_user * share), F32),
            vmem((nu, 8, n_user * share), F32),
            vmem((n_gen, 8, n_user * share), F32),
            dma((nu,)), dma((nu,)),
            dma((ng,)), dma((ng,)),
            dma((nu,)), dma((nu,)),
            dma((ng,)), dma((ng,)),
            dma((1,)), dma((1,)),
            dma((nu,)), dma((nu,)),
            dma((ng,)), dma((ng,)),
        ],
        compiler_params=pltpu.CompilerParams(
            collective_id=0, has_side_effects=True, vmem_limit_bytes=62 * 1024 * 1024
        ),
    )(states, norm_gain.reshape(1, width), split_columns(gate_weight), split_columns(up_weight),
      proj_weight, down_weight, private_rows, enc_weight,
      user_ids.reshape(rows, 1), user_ids.reshape(1, rows))


def shards(
    states,
    norm_gain,
    gate_weight,
    up_weight,
    down_weight,
    proj_weight,
    private_rows,
    enc_weight,
    user_ids,
):
    groups = states.shape[0] // STEPS
    row_total = private_rows.shape[0] * lax.axis_size("gen") * lax.axis_size("user")
    cand_total = groups * lax.axis_size("user") * lax.axis_size("cand")
    return fused(states, norm_gain, gate_weight, up_weight, proj_weight, down_weight,
                 private_rows, enc_weight, user_ids, cand_total / row_total)


def solution(mesh):
    return jax.shard_map(
        shards,
        mesh=mesh,
        in_specs=(
            P(("user", "cand"), None),
            P(),
            P("user", "gen"),
            P("user", "gen"),
            P("gen", "user"),
            P("gen", None),
            P(("gen", "user"), None),
            P(),
            P(("gen", "user")),
        ),
        out_specs=P(None, "cand", None),
        check_vma=False,
    )
```
